32 devices in a mesh: dp: 16 (over z, x, core), tensor: 2 (over y).
Axes of the slice: x: 2, y: 2, z: 4, core: 2. Of those that a mesh axis runs over, the one named last changes fastest.
Arguments:
- tokens: bfloat16 [2048, 1152], P('dp'), may hold values from -40 to 40
- conditions: bfloat16 [16, 1152], P('dp'), may hold values from -6 to 6
- mod_weight: bfloat16 [1152, 6912], P(None, 'dp'), may hold values from -0.1875 to 0.1875
- mod_bias: bfloat16 [6912], P('dp'), may hold values from -3 to 3
- qkv_weight: bfloat16 [1152, 3, 1152], P('dp', None, 'tensor'), may hold values from -0.1875 to 0.1875
- qv_bias: bfloat16 [2, 1152], P('tensor', 'dp'), may hold values from -3 to 3
- proj_weight: bfloat16 [1152, 1152], P('tensor', 'dp'), may hold values from -0.75 to 0.75
- proj_bias: bfloat16 [1152], P('dp'), may hold values from -3 to 3
- fc1_weight: bfloat16 [1152, 4608], P('dp', 'tensor'), may hold values from -0.1875 to 0.1875
- fc1_bias: bfloat16 [2, 2304], P('tensor', 'dp'), may hold values from -3 to 3
- fc2_weight: bfloat16 [4608, 1152], P('tensor', 'dp'), may hold values from -0.1875 to 0.1875
- fc2_bias: bfloat16 [1152], P('dp'), may hold values from -3 to 3
- cotangent: bfloat16 [2048, 1152], P('dp'), may hold values from -6 to 6
Outputs:
- block_out: bfloat16 [2048, 1152], P('dp')
- tokens_grad: float32 [2048, 1152], P('dp')
- conditions_grad: float32 [16, 1152], P('dp')
- mod_weight_grad: float32 [1152, 6912], P(None, 'dp')
- mod_bias_grad: float32 [6912], P('dp')
- qkv_weight_grad: float32 [1152, 3, 1152], P('dp', None, 'tensor')
- qv_bias_grad: float32 [2, 1152], P('tensor', 'dp')
- proj_weight_grad: float32 [1152, 1152], P('tensor', 'dp')
- proj_bias_grad: float32 [1152], P('dp')
- fc1_weight_grad: float32 [1152, 4608], P('dp', 'tensor')
- fc1_bias_grad: float32 [2, 2304], P('tensor', 'dp')
- fc2_weight_grad: float32 [4608, 1152], P('tensor', 'dp')
- fc2_bias_grad: float32 [1152], P('dp')
The draws below stay inside these ranges and needn't reach their ends.
All inputs are finite; a program needn't handle non-finite values.
Results may differ from the reference program's by a relative error of at most 0.015.
Values may be sent and summed in bfloat16 or wider, within the bound.
No kernel may reach another device: no remote copies, remote signals or barrier semaphores. Data moves between devices by JAX's collectives and lax.ppermute only.
A program may use at most 192 MiB of HBM per device.

```python
import math
import jax
import jax.numpy as jnp
from jax import lax

D = 1152
HEADS = 16
FF = 4608
SEQ = 128
HEAD = 72
LATENTS = 16
TOKENS = 2048
N_TENSOR = 2


def draw_tokens(key, part):
    key = jax.random.fold_in(key, 11)
    keys = jax.random.split(key, 3)
    row_scale = jnp.exp(jax.random.uniform(keys[0], (TOKENS, 1), jnp.float32, math.log(0.32), math.log(3.2)))
    col_scale = jnp.exp(jax.random.uniform(keys[1], (1, D), jnp.float32, math.log(0.32), math.log(3.2)))
    base = jnp.clip(jax.random.normal(keys[2], (TOKENS, D), jnp.float32), -3.5, 3.5)
    values = row_scale * col_scale * base
    return values.astype(jnp.bfloat16)


def with_spikes(array, own_key, source, target, blocks, factor):
    owner, partner = [(jnp.arange(array.shape[axis_at]) // (array.shape[axis_at] // blocks)).reshape([-1 if axis == axis_at else 1 for axis in range(array.ndim)]) for axis_at in (source, target)]
    chosen = jax.random.permutation(own_key, blocks)[partner]
    strong = (owner == chosen) | (owner == (partner + blocks // 2) % blocks)
    return jnp.where(strong, factor * array, array)


def levels(key, shape, pieces, smallest, top_value):
    def one(axis_at, parts):
        draws = jax.random.uniform(jax.random.fold_in(jax.random.fold_in(key, 6), axis_at), (parts,), jnp.float32, smallest / len(pieces), top_value / len(pieces))
        return jnp.repeat(jnp.exp(draws), shape[axis_at] // parts).reshape((-1,) + (1,) * (len(shape) - axis_at - 1))

    loudness = one(*pieces[0])
    for cut in pieces[1:]:
        loudness = loudness * one(*cut)
    return loudness


def noise(stream_key, extent, scale, limit, cuts=(), held_as=jnp.bfloat16):
    factor_of = levels(stream_key, extent, cuts, -0.22, 0.18) if cuts else 1.0
    drawn = jax.random.normal(stream_key, extent, jnp.float32) * scale * factor_of
    return jnp.minimum(jnp.maximum(drawn, -limit), limit).astype(held_as)


def bell_draw_with(rng, shape, deviation, reach, shards, heavy, kind=jnp.bfloat16):
    entries = deviation * jax.random.normal(rng, shape, jnp.float32)
    if shards:
        entries = entries * levels(rng, shape, shards, -0.22, 0.18)
    return jnp.clip(with_spikes(entries, jax.random.fold_in(rng, 3), *heavy), -reach, reach).astype(kind)


def setup_inputs(seed: int = 0) -> dict:
    key_of = jax.random.split(jax.random.key(seed), 14)
    return {
        "tokens": draw_tokens(jax.random.fold_in(key_of[13], 71), 0),
        "conditions": noise(key_of[1], (LATENTS, D), 1.0, 6.0, ((0, 16),)),
        "mod_weight": noise(key_of[2], (D, 6 * D), D ** -0.5, 0.1875, ((1, 16),)),
        "mod_bias": noise(key_of[3], (6 * D,), 0.5, 3.0, ((0, 16),)),
        "qkv_weight": noise(key_of[4], (D, 3, D), D ** -0.5, 0.1875, ((0, 16), (2, 2))),
        "qv_bias": noise(key_of[5], (N_TENSOR, 2 * D // N_TENSOR), 0.5, 3.0, ((0, 2), (1, 16))),
        "proj_weight": noise(key_of[6], (D, D), HEAD ** -0.5, 0.75, ((0, 2), (1, 16))),
        "proj_bias": noise(key_of[7], (D,), 0.5, 3.0, ((0, 16),)),
        "fc1_weight": noise(key_of[8], (D, FF), D ** -0.5, 0.1875, ((0, 16), (1, 2))),
        "fc1_bias": noise(key_of[9], (N_TENSOR, FF // N_TENSOR), 0.5, 3.0, ((0, 2), (1, 16))),
        "fc2_weight": noise(key_of[10], (FF, D), (FF // 4) ** -0.5, 0.1875, ((0, 2), (1, 16))),
        "fc2_bias": noise(key_of[11], (D,), 0.5, 3.0, ((0, 16),)),
        "cotangent": bell_draw_with(key_of[12], (TOKENS, D), 1.0, 6.0, ((0, 16),), (0, 1, 16, 2.0)),
    }


@jax.custom_vjp
def low(v):
    return lax.optimization_barrier(v.astype(jnp.bfloat16)).astype(jnp.float32)

@jax.custom_vjp
def low_back(v):
    return v

def low_keep(v):
    return (low(v), None)

def low_pass(kept, grad):
    return (grad,)

def back_keep(v):
    return (v, None)

def back_low(kept, grad):
    return (low(grad),)
low.defvjp(low_keep, low_pass)
low_back.defvjp(back_keep, back_low)
epsilon = 1e-06
highest = lax.Precision.HIGHEST

def layer_norm(values):
    row_mean = lax.optimization_barrier(jnp.mean(values, axis=-1, keepdims=True))
    centered = values - row_mean
    variance = lax.optimization_barrier(jnp.mean(centered * centered, axis=-1, keepdims=True))
    return centered * lax.rsqrt(variance + epsilon)

def matmul(left, right):
    return jnp.dot(left, right, precision=highest, preferred_element_type=jnp.float32)

def attend(triple):
    queries, keys_in, values = triple
    scores = jnp.einsum('qhd,khd->hqk', queries, keys_in, precision=highest) * HEAD ** (-0.5)
    weights = low(jax.nn.softmax(low_back(scores), axis=-1))
    return jnp.einsum('hqk,khd->qhd', weights, values, precision=highest)

def forward(params, inputs, conds):
    mod_weight, mod_bias, qkv_weight, qv_bias, proj_weight, proj_bias, fc1_weight, fc1_bias, fc2_weight, fc2_bias = params
    group = conds.shape[0]
    tensor_width = D // N_TENSOR
    silu_conds = low(jax.nn.silu(conds))
    modulation = low_back(matmul(silu_conds, mod_weight) + mod_bias).reshape(group, 1, 6, D)
    shift_attn = modulation[:, :, 0]
    scale_attn = modulation[:, :, 1]
    gate_attn = modulation[:, :, 2]
    shift_mlp = modulation[:, :, 3]
    scale_mlp = modulation[:, :, 4]
    gate_mlp = modulation[:, :, 5]
    states = inputs.reshape(group, SEQ, D)
    normed_one = low(layer_norm(states) * (1.0 + scale_attn) + shift_attn).reshape(group * SEQ, D)
    projected = matmul(normed_one, qkv_weight.reshape(D, 3 * D))
    query_bias = qv_bias[:, :tensor_width].reshape(D)
    value_bias = qv_bias[:, tensor_width:].reshape(D)
    queries = low(low_back(projected[:, :D]) + query_bias)
    keys_all = low(low_back(projected[:, D:2 * D]))
    values = low(low_back(projected[:, 2 * D:]) + value_bias)
    shape_heads = (group, SEQ, HEADS, HEAD)
    attended = lax.map(jax.checkpoint(attend), (queries.reshape(shape_heads), keys_all.reshape(shape_heads), values.reshape(shape_heads)))
    attended = low_back(low(attended.reshape(group * SEQ, D)))
    branch = low_back(matmul(attended, proj_weight)) + proj_bias
    hidden_state = states + gate_attn * branch.reshape(group, SEQ, D)
    normed_two = low(layer_norm(hidden_state) * (1.0 + scale_mlp) + shift_mlp).reshape(group * SEQ, D)
    pre_act = low_back(matmul(normed_two, fc1_weight)) + fc1_bias.reshape(FF)
    activated = low(jax.nn.gelu(pre_act, approximate=True))
    mlp_out = low_back(matmul(activated, fc2_weight)) + fc2_bias
    result = hidden_state + gate_mlp * mlp_out.reshape(group, SEQ, D)
    return result.reshape(group * SEQ, D)

def reference(tokens, conditions, mod_weight, mod_bias, qkv_weight, qv_bias, proj_weight, proj_bias, fc1_weight, fc1_bias, fc2_weight, fc2_bias, cotangent):
    params = tuple((item.astype(jnp.float32) for item in (mod_weight, mod_bias, qkv_weight, qv_bias, proj_weight, proj_bias, fc1_weight, fc1_bias, fc2_weight, fc2_bias)))
    group = min(LATENTS, max(1, 4096 // SEQ))
    rounds = LATENTS // group
    inputs = tokens.astype(jnp.float32).reshape(rounds, group * SEQ, D)
    conds = conditions.astype(jnp.float32).reshape(rounds, group, D)
    grads_in = cotangent.astype(jnp.float32).reshape(rounds, group * SEQ, D)

    def one_group(totals, item):
        part_inputs, part_conds, part_grads = item
        result, pull = jax.vjp(forward, params, part_inputs, part_conds)
        param_grads, input_grads, cond_grads = pull(part_grads)
        totals = jax.tree.map(jnp.add, totals, param_grads)
        return (totals, (result.astype(jnp.bfloat16), input_grads, cond_grads))
    zeros = jax.tree.map(jnp.zeros_like, params)
    totals, (outputs, input_grads, cond_grads) = lax.scan(one_group, zeros, (inputs, conds, grads_in))
    return (outputs.reshape(TOKENS, D), input_grads.reshape(TOKENS, D), cond_grads.reshape(LATENTS, D), totals[0], totals[1], totals[2], totals[3], totals[4], totals[5], totals[6], totals[7], totals[8], totals[9])
```

```python
import jax
import jax.numpy as jnp
from jax import lax
from jax.sharding import Mesh, PartitionSpec as P

HEAD = 72
EPSILON = 1e-06
GROUP = 4

bf16 = jnp.bfloat16
f32 = jnp.float32


def product(left, right, form):
    return jnp.einsum(form, left, right, preferred_element_type=f32)


def exchange(value, axis, mask=1):
    size = lax.axis_size(axis)
    return lax.ppermute(value, axis, [(i, i ^ mask) for i in range(size)])


def reorder(value, position):
    count = value.shape[0]
    bit = 1
    while bit < count:
        parts = value.reshape((count // (2 * bit), 2, bit) + value.shape[1:])
        flip = (position // bit) % 2 == 1
        first = jnp.where(flip, parts[:, 1], parts[:, 0])
        second = jnp.where(flip, parts[:, 0], parts[:, 1])
        value = jnp.stack([first, second], axis=1).reshape(value.shape)
        bit *= 2
    return value


def gather_dp(value):
    for axis in ("core", "xx"):
        value = jnp.concatenate([value, exchange(value, axis)], axis=0)
    mask = 1
    while mask < lax.axis_size("zz"):
        value = jnp.concatenate([value, exchange(value, "zz", mask)], axis=0)
        mask *= 2
    return value


def gather_four(value):
    value = jnp.concatenate([value, exchange(value, "xx")], axis=0)
    return jnp.concatenate([value, exchange(value, "core")], axis=0)


def gather_eight(value):
    over_y = exchange(value, "tensor")
    over_x = exchange(value, "xx")
    over_xy = exchange(value, ("xx", "tensor"), 3)
    near = jnp.concatenate([value, over_y, over_x, over_xy], axis=0)
    return jnp.concatenate([near, exchange(near, "core")], axis=0)


def scatter_eight(partial):
    half = partial.shape[0] // 2
    rows = half // 4
    near = partial[:half] + exchange(partial[half:].astype(bf16), "core").astype(f32)
    sent = near.astype(bf16)
    over_y = exchange(sent[rows : 2 * rows], "tensor")
    over_x = exchange(sent[2 * rows : 3 * rows], "xx")
    over_xy = exchange(sent[3 * rows :], ("xx", "tensor"), 3)
    return (near[:rows] + over_y.astype(f32)) + (over_x.astype(f32) + over_xy.astype(f32))


def swap_four(chunks, place):
    parts = [lax.dynamic_index_in_dim(chunks, place ^ d, 0, keepdims=False) for d in range(4)]
    got = [
        parts[0],
        exchange(parts[1], "core"),
        exchange(parts[2], "xx"),
        exchange(parts[3], ("xx", "core"), 3),
    ]
    return reorder(jnp.stack(got), place)


def norm(values):
    mean = jnp.mean(values, axis=-1, keepdims=True)
    centered = values - mean
    variance = jnp.mean(centered * centered, axis=-1, keepdims=True)
    inverse = lax.rsqrt(variance + EPSILON)
    return centered * inverse, inverse


def norm_back(grad, normed, inverse, scale):
    scaled = grad * (1.0 + scale)
    mean_scaled = jnp.mean(scaled, axis=-1, keepdims=True)
    mean_product = jnp.mean(scaled * normed, axis=-1, keepdims=True)
    return inverse * (scaled - mean_scaled - normed * mean_product)


def tanh_gelu(values):
    return jax.nn.gelu(values, approximate=True)


def local(
    tokens,
    conditions,
    mod_weight,
    mod_bias,
    qkv_weight,
    qv_bias,
    proj_weight,
    proj_bias,
    fc1_weight,
    fc1_bias,
    fc2_weight,
    fc2_bias,
    cotangent,
):
    seq, width = tokens.shape
    rows = seq // 2
    d_rows = qkv_weight.shape[0]
    t_width = qkv_weight.shape[2]
    hidden = fc1_weight.shape[1]
    feats = t_width // GROUP
    units = hidden // GROUP
    heads = feats // HEAD
    n_dp = width // d_rows
    factor = HEAD ** (-0.5)
    t = lax.axis_index("tensor")
    place = lax.axis_index("xx") * 2 + lax.axis_index("core")
    dp = lax.axis_index("zz") * GROUP + place

    qkv_chunks = qkv_weight.reshape(d_rows, 3, GROUP, feats).transpose(2, 0, 1, 3)
    qkv_chunks = qkv_chunks.reshape(GROUP, d_rows, 3 * feats)
    proj_chunks = proj_weight.T.reshape(d_rows, GROUP, feats).transpose(1, 0, 2)
    fc1_chunks = fc1_weight.reshape(d_rows, GROUP, units).transpose(1, 0, 2)
    fc2_chunks = fc2_weight.T.reshape(d_rows, GROUP, units).transpose(1, 0, 2)
    attn_part = swap_four(jnp.concatenate([qkv_chunks, proj_chunks], axis=2), place)
    mlp_part = swap_four(jnp.concatenate([fc1_chunks, fc2_chunks], axis=2), place)
    attn_part = attn_part.reshape(GROUP * d_rows, 4 * feats)
    mlp_part = mlp_part.reshape(GROUP * d_rows, 2 * units)
    attn_full = lax.all_gather(attn_part, "zz", axis=0, tiled=True)
    mlp_full = lax.all_gather(mlp_part, "zz", axis=0, tiled=True)
    qkv_full = attn_full[:, : 3 * feats]
    proj_full = attn_full[:, 3 * feats :]
    fc1_full = mlp_full[:, :units]
    fc2_full = mlp_full[:, units:]

    cond_values = conditions.astype(f32)
    silu_conds = jax.nn.silu(cond_values).astype(bf16)
    small = jnp.concatenate(
        [silu_conds, qv_bias, proj_bias[None], fc1_bias, fc2_bias[None]], axis=1
    )
    small = reorder(gather_dp(small), dp)
    n_qv, n_b, n_f = qv_bias.shape[1], proj_bias.shape[0], fc1_bias.shape[1]
    cuts = [width, width + n_qv, width + n_qv + n_b, width + n_qv + n_b + n_f]
    all_silu = small[:, : cuts[0]]
    qv_full = small[:, cuts[0] : cuts[1]].reshape(2, GROUP, feats).astype(f32)
    proj_bias_full = small[:, cuts[1] : cuts[2]].reshape(width).astype(f32)
    fc1_bias_full = small[:, cuts[2] : cuts[3]].reshape(GROUP, units).astype(f32)
    fc2_bias_full = small[:, cuts[3] :].reshape(width).astype(f32)
    qv_here = lax.dynamic_index_in_dim(qv_full, place, 1, keepdims=False)
    fc1_bias_here = lax.dynamic_index_in_dim(fc1_bias_full, place, 0, keepdims=False)
    mod_columns = product(all_silu, mod_weight, "ld,dc->lc") + mod_bias.astype(f32)
    mod_row = lax.all_to_all(
        mod_columns, ("zz", "xx", "core"), split_axis=0, concat_axis=1, tiled=True
    )
    mod_rows = gather_four(mod_row).reshape(GROUP, 6, width)
    shift_attn, scale_attn, gate_attn, shift_mlp, scale_mlp, gate_mlp = [
        mod_rows[:, i] for i in range(6)
    ]

    def own_order(value):
        first = lax.dynamic_slice_in_dim(value, t * rows, rows, 0)
        second = lax.dynamic_slice_in_dim(value, (1 - t) * rows, rows, 0)
        return jnp.concatenate([first, second], axis=0)

    def true_order(own, other):
        return jnp.where(
            t == 0,
            jnp.concatenate([own, other], axis=0),
            jnp.concatenate([other, own], axis=0),
        )

    tokens_own = own_order(tokens)
    cot_own = own_order(cotangent)
    tokens_all = gather_four(tokens_own).astype(f32).reshape(GROUP, seq, width)
    cot_all = gather_four(cot_own).astype(f32).reshape(GROUP, seq, width)
    inputs_half = tokens_own[:rows].astype(f32)
    grad_out_half = cot_own[:rows].astype(f32)

    total = GROUP * seq
    normed_one = norm(tokens_all)[0] * (1.0 + scale_attn[:, None]) + shift_attn[:, None]
    normed_one = normed_one.astype(bf16).reshape(total, width)
    projected = product(normed_one, qkv_full, "sd,df->sf")
    head_shape = (GROUP, seq, heads, HEAD)
    queries = (projected[:, :feats] + qv_here[0]).astype(bf16).reshape(head_shape)
    keys = projected[:, feats : 2 * feats].astype(bf16).reshape(head_shape)
    values = (projected[:, 2 * feats :] + qv_here[1]).astype(bf16).reshape(head_shape)
    scores = product(queries, keys, "lqhd,lkhd->lhqk") * factor
    exponent = jnp.exp(scores - jnp.max(scores, axis=-1, keepdims=True))
    probs = exponent / jnp.sum(exponent, axis=-1, keepdims=True)
    probs_low = probs.astype(bf16)
    attended = product(probs_low, values, "lhqk,lkhd->lqhd").astype(bf16).reshape(total, feats)
    branch_half = scatter_eight(product(attended, proj_full, "sf,df->sd")) + proj_bias_full
    hidden_half = inputs_half + gate_attn[0] * branch_half

    norm_two, inverse_two = norm(hidden_half)
    normed_two_half = (norm_two * (1.0 + scale_mlp[0]) + shift_mlp[0]).astype(bf16)
    normed_two = gather_eight(normed_two_half)
    pre_act = product(normed_two, fc1_full, "sd,df->sf") + fc1_bias_here
    activated = tanh_gelu(pre_act).astype(bf16)
    mlp_half = scatter_eight(product(activated, fc2_full, "sf,df->sd")) + fc2_bias_full
    block_half = (hidden_half + gate_mlp[0] * mlp_half).astype(bf16)

    def token_sum(value):
        parts = jnp.sum(value.reshape(2 * GROUP, rows, width), axis=1)
        pairs = parts[0::2] + parts[1::2]
        return (pairs[0] + pairs[1]) + (pairs[2] + pairs[3])

    grad_branch_mlp = (gate_mlp[:, None] * cot_all).reshape(total, width)
    fc2_bias_part = token_sum(grad_branch_mlp)
    grad_branch_low = grad_branch_mlp.astype(bf16)
    fc2_grad = product(grad_branch_low, activated, "sd,sf->df").astype(bf16)
    grad_activated = product(grad_branch_low, fc2_full, "sd,df->sf")
    grad_pre = jax.vjp(tanh_gelu, pre_act)[1](grad_activated)[0]
    fc1_bias_part = jnp.sum(grad_pre, axis=0)
    grad_pre_low = grad_pre.astype(bf16)
    fc1_grad = product(normed_two, grad_pre_low, "sd,sf->df").astype(bf16)
    mlp_grad = lax.psum_scatter(
        jnp.concatenate([fc1_grad, fc2_grad], axis=1), "zz", scatter_dimension=0, tiled=True
    )
    grad_normed_two = scatter_eight(product(grad_pre_low, fc1_full, "sf,df->sd"))
    grad_hidden_half = grad_out_half + norm_back(
        grad_normed_two, norm_two, inverse_two, scale_mlp[0]
    )
    grad_branch_half = (gate_attn[0] * grad_hidden_half).astype(bf16)

    grad_branch_all = gather_eight(grad_branch_half)
    proj_bias_part = token_sum(grad_branch_all.astype(f32))
    proj_grad = product(grad_branch_all, attended, "sd,sf->df").astype(bf16)
    grad_attended = product(grad_branch_all, proj_full, "sd,df->sf").astype(bf16)
    grad_attended = grad_attended.reshape(head_shape)
    grad_values = product(probs_low, grad_attended, "lhqk,lqhd->lkhd")
    grad_probs = product(grad_attended, values, "lqhd,lkhd->lhqk")
    grad_scores = probs * (grad_probs - jnp.sum(probs * grad_probs, axis=-1, keepdims=True))
    grad_scores = grad_scores.astype(bf16)
    grad_queries = product(grad_scores, keys, "lhqk,lkhd->lqhd") * factor
    grad_keys = product(grad_scores, queries, "lhqk,lqhd->lkhd") * factor
    grad_queries = grad_queries.reshape(total, feats)
    grad_keys = grad_keys.reshape(total, feats)
    grad_values = grad_values.reshape(total, feats)
    grad_qkv_low = jnp.concatenate([grad_queries, grad_keys, grad_values], axis=1).astype(bf16)
    qkv_grad = product(normed_one, grad_qkv_low, "sd,sf->df").astype(bf16)
    attn_grad = lax.psum_scatter(
        jnp.concatenate([qkv_grad, proj_grad], axis=1), "zz", scatter_dimension=0, tiled=True
    )
    grad_normed_one = scatter_eight(product(grad_qkv_low, qkv_full, "sf,df->sd"))
    norm_one, inverse_one = norm(inputs_half)
    tokens_grad_half = grad_hidden_half + norm_back(
        grad_normed_one, norm_one, inverse_one, scale_attn[0]
    )

    block_out = true_order(block_half, exchange(block_half, "tensor"))
    tokens_grad_half = tokens_grad_half.astype(bf16)
    tokens_grad = true_order(tokens_grad_half, exchange(tokens_grad_half, "tensor")).astype(f32)
    grad_mod = jnp.stack(
        [
            jnp.sum(grad_normed_one, axis=0),
            jnp.sum(grad_normed_one * norm_one, axis=0),
            jnp.sum(grad_hidden_half * branch_half, axis=0),
            jnp.sum(grad_normed_two, axis=0),
            jnp.sum(grad_normed_two * norm_two, axis=0),
            jnp.sum(grad_out_half * mlp_half, axis=0),
        ]
    ).reshape(1, 6 * width)
    grad_mod = (grad_mod + exchange(grad_mod, "tensor")).astype(bf16)
    grad_mod_columns = lax.all_to_all(
        grad_mod, ("zz", "xx", "core"), split_axis=1, concat_axis=0, tiled=True
    )
    mod_bias_grad = jnp.sum(grad_mod_columns.astype(f32), axis=0)
    mod_weight_grad = product(all_silu, grad_mod_columns, "ld,lc->dc")
    grad_silu = lax.psum_scatter(
        product(grad_mod_columns, mod_weight, "lc,dc->ld"),
        ("zz", "xx", "core"),
        scatter_dimension=0,
        tiled=True,
    )
    conditions_grad = jax.vjp(jax.nn.silu, cond_values)[1](grad_silu)[0]

    biases = jnp.concatenate(
        [
            jnp.sum(grad_queries, axis=0),
            jnp.sum(grad_values, axis=0),
            fc1_bias_part,
            proj_bias_part,
            fc2_bias_part,
        ]
    )
    biases = lax.psum(biases, "zz")
    own = 2 * feats + units
    group_biases = biases[None, :own]
    for axis in ("core", "xx"):
        group_biases = jnp.concatenate([group_biases, exchange(group_biases, axis)], axis=0)
    group_biases = reorder(group_biases, place)
    qv_all = jnp.concatenate(
        [group_biases[:, :feats].reshape(-1), group_biases[:, feats : 2 * feats].reshape(-1)]
    )
    fc1_all = group_biases[:, 2 * feats :].reshape(-1)
    proj_all = biases[own : own + width]
    fc2_all = biases[own + width :]

    def piece(vector):
        size = vector.shape[0] // n_dp
        return lax.dynamic_slice_in_dim(vector, dp * size, size, 0)

    mlp_grad = swap_four(mlp_grad.reshape(GROUP, d_rows, 2 * units), place).astype(f32)
    attn_grad = swap_four(attn_grad.reshape(GROUP, d_rows, 4 * feats), place).astype(f32)
    fc1_weight_grad = mlp_grad[:, :, :units].transpose(1, 0, 2).reshape(d_rows, hidden)
    fc2_weight_grad = mlp_grad[:, :, units:].transpose(1, 0, 2).reshape(d_rows, hidden).T
    qkv_weight_grad = attn_grad[:, :, : 3 * feats].reshape(GROUP, d_rows, 3, feats)
    qkv_weight_grad = qkv_weight_grad.transpose(1, 2, 0, 3).reshape(d_rows, 3, t_width)
    proj_weight_grad = attn_grad[:, :, 3 * feats :].transpose(1, 0, 2).reshape(d_rows, t_width).T
    return (
        block_out,
        tokens_grad,
        conditions_grad,
        mod_weight_grad,
        mod_bias_grad,
        qkv_weight_grad,
        piece(qv_all)[None],
        proj_weight_grad,
        piece(proj_all),
        fc1_weight_grad,
        piece(fc1_all)[None],
        fc2_weight_grad,
        piece(fc2_all),
    )


def solution(mesh):
    n_dp, n_tensor = mesh.shape["dp"], mesh.shape["tensor"]
    cut = Mesh(
        mesh.devices.reshape(n_dp // GROUP, 2, 2, n_tensor), ("zz", "xx", "core", "tensor")
    )
    dp = ("zz", "xx", "core")
    return jax.shard_map(
        local,
        mesh=cut,
        in_specs=(
            P(dp, None),
            P(dp, None),
            P(None, dp),
            P(dp),
            P(dp, None, "tensor"),
            P("tensor", dp),
            P("tensor", dp),
            P(dp),
            P(dp, "tensor"),
            P("tensor", dp),
            P("tensor", dp),
            P(dp),
            P(dp, None),
        ),
        out_specs=(
            P(dp, None),
            P(dp, None),
            P(dp, None),
            P(None, dp),
            P(dp),
            P(dp, None, "tensor"),
            P("tensor", dp),
            P("tensor", dp),
            P(dp),
            P(dp, "tensor"),
            P("tensor", dp),
            P("tensor", dp),
            P(dp),
        ),
        check_vma=False,
    )
```

```python
import jax
import jax.numpy as jnp
from jax import lax
from jax.experimental import pallas as pl
from jax.experimental.pallas import tpu as pltpu
from jax.sharding import Mesh, PartitionSpec as P

HEAD = 72
EPSILON = 1e-06
GROUP = 4
ROOT = 0.7978845608028654
VMEM_LIMIT = 48 * 1024 * 1024

bf16 = jnp.bfloat16
f32 = jnp.float32


def product(left, right, form):
    return jnp.einsum(form, left, right, preferred_element_type=f32)


def exchange(value, axis, mask=1):
    size = lax.axis_size(axis)
    return lax.ppermute(value, axis, [(i, i ^ mask) for i in range(size)])


def reorder(value, position):
    count = value.shape[0]
    bit = 1
    while bit < count:
        parts = value.reshape((count // (2 * bit), 2, bit) + value.shape[1:])
        flip = (position // bit) % 2 == 1
        first = jnp.where(flip, parts[:, 1], parts[:, 0])
        second = jnp.where(flip, parts[:, 0], parts[:, 1])
        value = jnp.stack([first, second], axis=1).reshape(value.shape)
        bit *= 2
    return value


def after(value, *others):
    def nothing(*refs):
        pass

    return pl.pallas_call(
        nothing,
        out_shape=jax.ShapeDtypeStruct(value.shape, value.dtype),
        in_specs=[pl.BlockSpec(memory_space=pl.ANY)] * (1 + len(others)),
        out_specs=pl.BlockSpec(memory_space=pl.ANY),
        input_output_aliases={0: 0},
    )(value, *others)


def scatter_dp(value):
    masks = []
    mask = 1
    while mask < lax.axis_size("zz"):
        masks.append(("zz", mask))
        mask *= 2
    for axis, mask in masks[::-1] + [("xx", 1), ("core", 1)]:
        half = value.shape[0] // 2
        value = value[:half] + exchange(value[half:], axis, mask)
    return value


def sum_zz(value):
    mask = 1
    while mask < lax.axis_size("zz"):
        value = value + exchange(value, "zz", mask)
        mask *= 2
    return value


def gather_dp(value):
    for axis in ("core", "xx"):
        value = jnp.concatenate([value, exchange(value, axis)], axis=0)
    mask = 1
    while mask < lax.axis_size("zz"):
        value = jnp.concatenate([value, exchange(value, "zz", mask)], axis=0)
        mask *= 2
    return value


def gather_four(value):
    value = jnp.concatenate([value, exchange(value, "xx")], axis=0)
    return jnp.concatenate([value, exchange(value, "core")], axis=0)


def gather_eight(value):
    over_y = exchange(value, "tensor")
    over_x = exchange(value, "xx")
    over_xy = exchange(value, ("xx", "tensor"), 3)
    near = jnp.concatenate([value, over_y, over_x, over_xy], axis=0)
    return jnp.concatenate([near, exchange(near, "core")], axis=0)


def scatter_eight(keep, send):
    rows = keep.shape[0] // 4
    near = keep + exchange(send, "core").astype(f32)
    sent = near.astype(bf16)
    over_y = exchange(sent[rows : 2 * rows], "tensor")
    over_x = exchange(sent[2 * rows : 3 * rows], "xx")
    over_xy = exchange(sent[3 * rows :], ("xx", "tensor"), 3)
    return (near[:rows] + over_y.astype(f32)) + (over_x.astype(f32) + over_xy.astype(f32))


def swap_four(chunks, place):
    parts = [lax.dynamic_index_in_dim(chunks, place ^ d, 0, keepdims=False) for d in range(4)]
    got = [
        parts[0],
        exchange(parts[1], "core"),
        exchange(parts[2], "xx"),
        exchange(parts[3], ("xx", "core"), 3),
    ]
    return reorder(jnp.stack(got), place)


def norm(values):
    mean = jnp.mean(values, axis=-1, keepdims=True)
    centered = values - mean
    variance = jnp.mean(centered * centered, axis=-1, keepdims=True)
    inverse = lax.rsqrt(variance + EPSILON)
    return centered * inverse, inverse


def norm_back(grad, normed, inverse, scale):
    scaled = grad * (1.0 + scale)
    mean_scaled = jnp.mean(scaled, axis=-1, keepdims=True)
    mean_product = jnp.mean(scaled * normed, axis=-1, keepdims=True)
    return inverse * (scaled - mean_scaled - normed * mean_product)


def transposed_dot(left, right):
    return lax.dot_general(left, right, (((0,), (0,)), ((), ())), preferred_element_type=f32)


def dot_rows(left, right):
    return lax.dot_general(left, right, (((1,), (1,)), ((), ())), preferred_element_type=f32)


def dot(left, right):
    return lax.dot_general(left, right, (((1,), (0,)), ((), ())), preferred_element_type=f32)


def call(kernel, outs, args, flops=0):
    return pl.pallas_call(
        kernel,
        out_shape=[jax.ShapeDtypeStruct(shape, dtype) for shape, dtype in outs],
        in_specs=[pl.BlockSpec(memory_space=pltpu.VMEM)] * len(args),
        out_specs=[pl.BlockSpec(memory_space=pltpu.VMEM)] * len(outs),
        compiler_params=pltpu.CompilerParams(vmem_limit_bytes=VMEM_LIMIT),
        cost_estimate=pl.CostEstimate(flops=flops, bytes_accessed=0, transcendentals=0),
    )(*args)


def head_masks(feats):
    lane = lax.broadcasted_iota(jnp.int32, (1, feats), 1)
    return [(lane >= h * HEAD) & (lane < (h + 1) * HEAD) for h in range(feats // HEAD)]


def only(mask, value):
    return jnp.where(mask, value, jnp.zeros_like(value))


def split_store(keep_ref, send_ref, value):
    half = value.shape[0] // 2
    keep_ref[...] = value[:half]
    send_ref[...] = value[half:].astype(bf16)


def attention_forward(tokens, shift, scale, weights, biases):
    total, width = tokens.shape
    feats = biases.shape[1]
    seq = total // GROUP
    factor = HEAD ** (-0.5)

    def kernel(tok, sh, sc, w, b, normed, q_out, k_out, v_out, att, keep, send):
        for i in range(GROUP):
            rows = slice(i * seq, (i + 1) * seq)
            value = norm(tok[rows, :].astype(f32))[0]
            normed[rows, :] = (value * (1.0 + sc[i : i + 1, :]) + sh[i : i + 1, :]).astype(bf16)
        projected = dot(normed[...], w[:, : 3 * feats])
        q_out[...] = (projected[:, :feats] + b[0:1, :]).astype(bf16)
        k_out[...] = projected[:, feats : 2 * feats].astype(bf16)
        v_out[...] = (projected[:, 2 * feats :] + b[1:2, :]).astype(bf16)
        masks = head_masks(feats)
        for i in range(GROUP):
            rows = slice(i * seq, (i + 1) * seq)
            q, k, v = q_out[rows, :], k_out[rows, :], v_out[rows, :]
            result = jnp.zeros((seq, feats), f32)
            for mask in masks:
                probs = softmax(dot_rows(only(mask, q), k) * factor)
                result += dot(probs.astype(bf16), only(mask, v))
            att[rows, :] = result.astype(bf16)
        split_store(keep, send, dot_rows(att[...], w[:, 3 * feats :]))

    return call(
        kernel,
        [
            ((total, width), bf16),
            ((total, feats), bf16),
            ((total, feats), bf16),
            ((total, feats), bf16),
            ((total, feats), bf16),
            ((total // 2, width), f32),
            ((total // 2, width), bf16),
        ],
        (tokens, shift, scale, weights, biases),
    )


def softmax(scores):
    exponent = jnp.exp(scores - jnp.max(scores, axis=-1, keepdims=True))
    return exponent / jnp.sum(exponent, axis=-1, keepdims=True)


def attention_backward(grad_branch, normed, q_all, k_all, v_all, att, weights):
    total, width = normed.shape
    feats = q_all.shape[1]
    seq = total // GROUP
    factor = HEAD ** (-0.5)

    def kernel(g, n, q_in, k_in, v_in, a, w, grads, keep, send, bias, grad_in):
        masks = head_masks(feats)
        grad_att = dot(g[...], w[:, 3 * feats :]).astype(bf16)
        q_sum = jnp.zeros((1, feats), f32)
        v_sum = jnp.zeros((1, feats), f32)
        for i in range(GROUP):
            rows = slice(i * seq, (i + 1) * seq)
            q, k, v = q_in[rows, :], k_in[rows, :], v_in[rows, :]
            ga = grad_att[rows, :]
            gq = jnp.zeros((seq, feats), f32)
            gk = jnp.zeros((seq, feats), f32)
            gv = jnp.zeros((seq, feats), f32)
            for mask in masks:
                probs = softmax(dot_rows(only(mask, q), k) * factor)
                gv += only(mask, transposed_dot(probs.astype(bf16), ga))
                gp = dot_rows(only(mask, ga), v)
                gs = probs * (gp - jnp.sum(probs * gp, axis=-1, keepdims=True))
                gs = gs.astype(bf16)
                gq += only(mask, dot(gs, k))
                gk += only(mask, transposed_dot(gs, q))
            gq, gk = gq * factor, gk * factor
            q_sum += jnp.sum(gq, axis=0, keepdims=True)
            v_sum += jnp.sum(gv, axis=0, keepdims=True)
            grad_in[rows, :] = jnp.concatenate([gq, gk, gv], axis=1).astype(bf16)
        bias[0:1, :] = q_sum
        bias[1:2, :] = v_sum
        split_store(keep, send, dot_rows(grad_in[...], w[:, : 3 * feats]))
        grads[:, : 3 * feats] = transposed_dot(n[...], grad_in[...]).astype(bf16)
        grads[:, 3 * feats :] = transposed_dot(g[...], a[...]).astype(bf16)

    return call(
        kernel,
        [
            ((width, 4 * feats), bf16),
            ((total // 2, width), f32),
            ((total // 2, width), bf16),
            ((2, feats), f32),
            ((total, 3 * feats), bf16),
        ],
        (grad_branch, normed, q_all, k_all, v_all, att, weights),
    )


def feed_forward(normed, weights, bias, cot, gate):
    total, width = normed.shape
    units = weights.shape[1] // 2
    seq = total // GROUP

    def kernel(n, w, b, c, gt, grads, keep, send, out_keep, out_send, bias_out, fc2_out, grad_out):
        sums = []
        for i in range(2 * GROUP):
            rows = slice(i * seq // 2, (i + 1) * seq // 2)
            value = c[rows, :].astype(f32) * gt[i // 2 : i // 2 + 1, :]
            sums.append(jnp.sum(value, axis=0, keepdims=True))
            grad_out[rows, :] = value.astype(bf16)
        pairs = [sums[2 * i] + sums[2 * i + 1] for i in range(GROUP)]
        fc2_out[...] = (pairs[0] + pairs[1]) + (pairs[2] + pairs[3])
        pre = dot(n[...], w[:, :units]) + b[...]
        inner = ROOT * (pre + 0.044715 * (pre * pre * pre))
        tanh = jnp.tanh(inner)
        act = (0.5 * pre * (1.0 + tanh)).astype(bf16)
        slope = 0.5 * (1.0 + tanh) + 0.5 * pre * (1.0 - tanh * tanh) * (
            ROOT * (1.0 + 3 * 0.044715 * (pre * pre))
        )
        grad_pre = dot(grad_out[...], w[:, units:]) * slope
        bias_out[...] = jnp.sum(grad_pre, axis=0, keepdims=True)
        grad_pre = grad_pre.astype(bf16)
        grads[:, units:] = transposed_dot(grad_out[...], act).astype(bf16)
        grads[:, :units] = transposed_dot(n[...], grad_pre).astype(bf16)
        split_store(keep, send, dot_rows(grad_pre, w[:, :units]))
        split_store(out_keep, out_send, dot_rows(act, w[:, units:]))

    return call(
        kernel,
        [
            ((width, 2 * units), bf16),
            ((total // 2, width), f32),
            ((total // 2, width), bf16),
            ((total // 2, width), f32),
            ((total // 2, width), bf16),
            ((1, units), f32),
            ((1, width), f32),
            ((total, width), bf16),
        ],
        (normed, weights, bias, cot, gate),
    )


def local(
    tokens,
    conditions,
    mod_weight,
    mod_bias,
    qkv_weight,
    qv_bias,
    proj_weight,
    proj_bias,
    fc1_weight,
    fc1_bias,
    fc2_weight,
    fc2_bias,
    cotangent,
):
    seq, width = tokens.shape
    rows = seq // 2
    d_rows = qkv_weight.shape[0]
    t_width = qkv_weight.shape[2]
    hidden = fc1_weight.shape[1]
    feats = t_width // GROUP
    units = hidden // GROUP
    n_dp = width // d_rows
    t = lax.axis_index("tensor")
    place = lax.axis_index("xx") * 2 + lax.axis_index("core")
    dp = lax.axis_index("zz") * GROUP + place

    qkv_chunks = qkv_weight.reshape(d_rows, 3, GROUP, feats).transpose(2, 0, 1, 3)
    qkv_chunks = qkv_chunks.reshape(GROUP, d_rows, 3 * feats)
    proj_chunks = proj_weight.T.reshape(d_rows, GROUP, feats).transpose(1, 0, 2)
    fc1_chunks = fc1_weight.reshape(d_rows, GROUP, units).transpose(1, 0, 2)
    fc2_chunks = fc2_weight.T.reshape(d_rows, GROUP, units).transpose(1, 0, 2)
    attn_chunks = jnp.concatenate([qkv_chunks, proj_chunks], axis=2)
    attn_part = swap_four(attn_chunks, place)
    mlp_part = swap_four(jnp.concatenate([fc1_chunks, fc2_chunks], axis=2), place)
    attn_part = attn_part.reshape(GROUP * d_rows, 4 * feats)
    mlp_part = mlp_part.reshape(GROUP * d_rows, 2 * units)
    attn_full = lax.all_gather(attn_part, "zz", axis=0, tiled=True)
    mlp_full = lax.all_gather(mlp_part, "zz", axis=0, tiled=True)

    cond_values = after(conditions, attn_chunks).astype(f32)
    silu_conds = jax.nn.silu(cond_values).astype(bf16)
    small = jnp.concatenate(
        [silu_conds, qv_bias, proj_bias[None], fc1_bias, fc2_bias[None]], axis=1
    )
    small = reorder(gather_dp(small), dp)
    n_qv, n_b, n_f = qv_bias.shape[1], proj_bias.shape[0], fc1_bias.shape[1]
    cuts = [width, width + n_qv, width + n_qv + n_b, width + n_qv + n_b + n_f]
    all_silu = small[:, : cuts[0]]
    qv_full = small[:, cuts[0] : cuts[1]].reshape(2, GROUP, feats).astype(f32)
    proj_bias_full = small[:, cuts[1] : cuts[2]].reshape(width).astype(f32)
    fc1_bias_full = small[:, cuts[2] : cuts[3]].reshape(GROUP, units).astype(f32)
    fc2_bias_full = small[:, cuts[3] :].reshape(width).astype(f32)
    qv_here = lax.dynamic_index_in_dim(qv_full, place, 1, keepdims=False)
    fc1_bias_here = lax.dynamic_index_in_dim(fc1_bias_full, place, 0, keepdims=False)
    mod_columns = product(all_silu, mod_weight, "ld,dc->lc") + mod_bias.astype(f32)
    mod_row = lax.all_to_all(
        mod_columns, ("zz", "xx", "core"), split_axis=0, concat_axis=1, tiled=True
    )
    mod_rows = gather_four(mod_row).reshape(GROUP, 6, width)
    shift_attn, scale_attn, gate_attn, shift_mlp, scale_mlp, gate_mlp = [
        mod_rows[:, i] for i in range(6)
    ]

    def own_order(value):
        first = lax.dynamic_slice_in_dim(value, t * rows, rows, 0)
        second = lax.dynamic_slice_in_dim(value, (1 - t) * rows, rows, 0)
        return jnp.concatenate([first, second], axis=0)

    def true_order(own, other):
        return jnp.where(
            t == 0,
            jnp.concatenate([own, other], axis=0),
            jnp.concatenate([other, own], axis=0),
        )

    tokens_own = own_order(tokens)
    cot_own = own_order(cotangent)
    tokens_low = gather_four(tokens_own)
    cot_low = gather_four(cot_own)
    inputs_half = tokens_own[:rows].astype(f32)
    grad_out_half = cot_own[:rows].astype(f32)

    total = GROUP * seq
    normed_one, queries, keys, values, attended, keep, send = attention_forward(
        tokens_low, shift_attn, scale_attn, attn_full, qv_here
    )
    branch_half = scatter_eight(keep, send) + proj_bias_full
    hidden_half = inputs_half + gate_attn[0] * branch_half

    norm_two, inverse_two = norm(hidden_half)
    normed_two_half = (norm_two * (1.0 + scale_mlp[0]) + shift_mlp[0]).astype(bf16)
    normed_two_half = after(normed_two_half, cot_low)
    normed_two = gather_eight(normed_two_half)
    mlp_grad, keep, send, out_keep, out_send, fc1_bias_part, fc2_bias_part, _ = feed_forward(
        normed_two, mlp_full, fc1_bias_here[None], cot_low, gate_mlp
    )
    mlp_grad = lax.psum_scatter(mlp_grad, "zz", scatter_dimension=0, tiled=True)
    grad_normed_two = scatter_eight(keep, send)
    grad_hidden_half = grad_out_half + norm_back(
        grad_normed_two, norm_two, inverse_two, scale_mlp[0]
    )
    grad_branch_half = (gate_attn[0] * grad_hidden_half).astype(bf16)
    grad_branch_all = gather_eight(grad_branch_half)

    mlp_half = scatter_eight(out_keep, after(out_send, grad_branch_half)) + fc2_bias_full
    block_half = (hidden_half + gate_mlp[0] * mlp_half).astype(bf16)

    def token_sum(value):
        parts = jnp.sum(value.reshape(2 * GROUP, rows, width), axis=1)
        pairs = parts[0::2] + parts[1::2]
        return (pairs[0] + pairs[1]) + (pairs[2] + pairs[3])

    proj_bias_part = token_sum(grad_branch_all.astype(f32))
    attn_grad, keep, send, qv_bias_part, _ = attention_backward(
        grad_branch_all, normed_one, queries, keys, values, attended, attn_full
    )
    attn_grad = lax.psum_scatter(
        after(attn_grad, mlp_grad), "zz", scatter_dimension=0, tiled=True
    )
    grad_normed_one = scatter_eight(keep, send)
    norm_one, inverse_one = norm(inputs_half)
    tokens_grad_half = grad_hidden_half + norm_back(
        grad_normed_one, norm_one, inverse_one, scale_attn[0]
    )

    block_out = true_order(block_half, exchange(block_half, "tensor"))
    tokens_grad_half = tokens_grad_half.astype(bf16)
    tokens_grad = true_order(tokens_grad_half, exchange(tokens_grad_half, "tensor")).astype(f32)
    grad_mod = jnp.stack(
        [
            jnp.sum(grad_normed_one, axis=0),
            jnp.sum(grad_normed_one * norm_one, axis=0),
            jnp.sum(grad_hidden_half * branch_half, axis=0),
            jnp.sum(grad_normed_two, axis=0),
            jnp.sum(grad_normed_two * norm_two, axis=0),
            jnp.sum(grad_out_half * mlp_half, axis=0),
        ]
    ).reshape(1, 6 * width)
    grad_mod = (grad_mod + exchange(grad_mod, "tensor")).astype(bf16)
    grad_mod_columns = lax.all_to_all(
        grad_mod, ("zz", "xx", "core"), split_axis=1, concat_axis=0, tiled=True
    )
    mod_bias_grad = jnp.sum(grad_mod_columns.astype(f32), axis=0)
    mod_weight_grad = product(all_silu, grad_mod_columns, "ld,lc->dc")
    grad_silu = scatter_dp(reorder(product(grad_mod_columns, mod_weight, "lc,dc->ld"), dp))
    conditions_grad = jax.vjp(jax.nn.silu, cond_values)[1](grad_silu)[0]

    biases = jnp.concatenate(
        [
            qv_bias_part.reshape(-1),
            fc1_bias_part[0],
            proj_bias_part,
            fc2_bias_part[0],
        ]
    )
    biases = sum_zz(biases)
    own = 2 * feats + units
    group_biases = biases[None, :own]
    for axis in ("core", "xx"):
        group_biases = jnp.concatenate([group_biases, exchange(group_biases, axis)], axis=0)
    group_biases = reorder(group_biases, place)
    qv_all = jnp.concatenate(
        [group_biases[:, :feats].reshape(-1), group_biases[:, feats : 2 * feats].reshape(-1)]
    )
    fc1_all = group_biases[:, 2 * feats :].reshape(-1)
    proj_all = biases[own : own + width]
    fc2_all = biases[own + width :]

    def piece(vector):
        size = vector.shape[0] // n_dp
        return lax.dynamic_slice_in_dim(vector, dp * size, size, 0)

    mlp_grad = swap_four(mlp_grad.reshape(GROUP, d_rows, 2 * units), place).astype(f32)
    attn_grad = swap_four(attn_grad.reshape(GROUP, d_rows, 4 * feats), place).astype(f32)
    fc1_weight_grad = mlp_grad[:, :, :units].transpose(1, 0, 2).reshape(d_rows, hidden)
    fc2_weight_grad = mlp_grad[:, :, units:].transpose(1, 0, 2).reshape(d_rows, hidden).T
    qkv_weight_grad = attn_grad[:, :, : 3 * feats].reshape(GROUP, d_rows, 3, feats)
    qkv_weight_grad = qkv_weight_grad.transpose(1, 2, 0, 3).reshape(d_rows, 3, t_width)
    proj_weight_grad = attn_grad[:, :, 3 * feats :].transpose(1, 0, 2).reshape(d_rows, t_width).T
    return (
        block_out,
        tokens_grad,
        conditions_grad,
        mod_weight_grad,
        mod_bias_grad,
        qkv_weight_grad,
        piece(qv_all)[None],
        proj_weight_grad,
        piece(proj_all),
        fc1_weight_grad,
        piece(fc1_all)[None],
        fc2_weight_grad,
        piece(fc2_all),
    )


def solution(mesh):
    n_dp, n_tensor = mesh.shape["dp"], mesh.shape["tensor"]
    cut = Mesh(
        mesh.devices.reshape(n_dp // GROUP, 2, 2, n_tensor), ("zz", "xx", "core", "tensor")
    )
    dp = ("zz", "xx", "core")
    return jax.shard_map(
        local,
        mesh=cut,
        in_specs=(
            P(dp, None),
            P(dp, None),
            P(None, dp),
            P(dp),
            P(dp, None, "tensor"),
            P("tensor", dp),
            P("tensor", dp),
            P(dp),
            P(dp, "tensor"),
            P("tensor", dp),
            P("tensor", dp),
            P(dp),
            P(dp, None),
        ),
        out_specs=(
            P(dp, None),
            P(dp, None),
            P(dp, None),
            P(None, dp),
            P(dp),
            P(dp, None, "tensor"),
            P("tensor", dp),
            P("tensor", dp),
            P(dp),
            P(dp, "tensor"),
            P("tensor", dp),
            P("tensor", dp),
            P(dp),
        ),
        check_vma=False,
    )
```

```python
import jax
import jax.numpy as jnp
from jax import lax
from jax.experimental import pallas as pl
from jax.experimental.pallas import tpu as pltpu
from jax.sharding import Mesh, PartitionSpec as P

HEAD = 72
EPSILON = 1e-06
GROUP = 4
ROOT = 0.7978845608028654
VMEM_LIMIT = 48 * 1024 * 1024

bf16 = jnp.bfloat16
f32 = jnp.float32


def product(left, right, form):
    return jnp.einsum(form, left, right, preferred_element_type=f32)


def exchange(value, axis, mask=1):
    size = lax.axis_size(axis)
    return lax.ppermute(value, axis, [(i, i ^ mask) for i in range(size)])


def reorder(value, position):
    count = value.shape[0]
    bit = 1
    while bit < count:
        parts = value.reshape((count // (2 * bit), 2, bit) + value.shape[1:])
        flip = (position // bit) % 2 == 1
        first = jnp.where(flip, parts[:, 1], parts[:, 0])
        second = jnp.where(flip, parts[:, 0], parts[:, 1])
        value = jnp.stack([first, second], axis=1).reshape(value.shape)
        bit *= 2
    return value


def after(value, *others):
    def nothing(*refs):
        pass

    return pl.pallas_call(
        nothing,
        out_shape=jax.ShapeDtypeStruct(value.shape, value.dtype),
        in_specs=[pl.BlockSpec(memory_space=pl.ANY)] * (1 + len(others)),
        out_specs=pl.BlockSpec(memory_space=pl.ANY),
        input_output_aliases={0: 0},
    )(value, *others)


def send_four(parts):
    return [
        parts[0],
        exchange(parts[1], "core"),
        exchange(parts[2], "xx"),
        exchange(parts[3], ("xx", "core"), 3),
    ]


def send_zz(parts):
    return [parts[0]] + [exchange(parts[m], "zz", m) for m in range(1, len(parts))]


def gather_dp(value):
    four = jnp.concatenate(send_four([value] * GROUP), axis=0)
    return jnp.concatenate(send_zz([four] * lax.axis_size("zz")), axis=0)


def scatter_dp(value, *others):
    steps = lax.axis_size("zz")
    four = sum(send_zz([value[m * GROUP : (m + 1) * GROUP] for m in range(steps)]))
    four = after(four, *others)
    return sum(send_four([four[d : d + 1] for d in range(GROUP)]))


def gather_four(value):
    near = jnp.concatenate([value, exchange(value, "xx")], axis=0)
    return near, exchange(near, "core")


def gather_eight(value, *others):
    parts = send_plane([value] * 4)

    def kernel(*refs):
        rows = value.shape[0]
        for i in range(4):
            refs[4][i * rows : (i + 1) * rows, :] = refs[i][...]

    near = call(kernel, [((4 * value.shape[0], value.shape[1]), bf16)], parts)[0]
    if others:
        near = after(near, *others)
    return near, exchange(near, "core")


def send_plane(parts):
    return [
        parts[0],
        exchange(parts[1], "tensor"),
        exchange(parts[2], "xx"),
        exchange(parts[3], ("xx", "tensor"), 3),
    ]


def scatter_eight(keep, send):
    rows = keep.shape[0] // 4
    shape = (rows, keep.shape[1])

    def kernel(a, b, own, *sent):
        own[...] = a[:rows, :] + b[:rows, :].astype(f32)
        for i in range(1, 4):
            part = slice(i * rows, (i + 1) * rows)
            sent[i - 1][...] = (a[part, :] + b[part, :].astype(f32)).astype(bf16)

    got = exchange(send, "core")
    return send_plane(call(kernel, [(shape, f32)] + [(shape, bf16)] * 3, (keep, got)))


def total_of(refs):
    own, one, two, three = [ref[...].astype(f32) for ref in refs]
    return (own + one) + (two + three)


def norm(values):
    mean = jnp.mean(values, axis=-1, keepdims=True)
    centered = values - mean
    variance = jnp.mean(centered * centered, axis=-1, keepdims=True)
    inverse = lax.rsqrt(variance + EPSILON)
    return centered * inverse, inverse


def norm_back(grad, normed, inverse, scale):
    scaled = grad * (1.0 + scale)
    mean_scaled = jnp.mean(scaled, axis=-1, keepdims=True)
    mean_product = jnp.mean(scaled * normed, axis=-1, keepdims=True)
    return inverse * (scaled - mean_scaled - normed * mean_product)


def transposed_dot(left, right):
    return lax.dot_general(left, right, (((0,), (0,)), ((), ())), preferred_element_type=f32)


def dot_rows(left, right):
    return lax.dot_general(left, right, (((1,), (1,)), ((), ())), preferred_element_type=f32)


def dot(left, right):
    return lax.dot_general(left, right, (((1,), (0,)), ((), ())), preferred_element_type=f32)


def call(kernel, outs, args, flops=0):
    return pl.pallas_call(
        kernel,
        out_shape=[jax.ShapeDtypeStruct(shape, dtype) for shape, dtype in outs],
        in_specs=[pl.BlockSpec(memory_space=pltpu.VMEM)] * len(args),
        out_specs=[pl.BlockSpec(memory_space=pltpu.VMEM)] * len(outs),
        compiler_params=pltpu.CompilerParams(vmem_limit_bytes=VMEM_LIMIT),
        cost_estimate=pl.CostEstimate(flops=flops, bytes_accessed=0, transcendentals=0),
    )(*args)


def place_call(kernel, outs, args, place, *scratch):
    return pl.pallas_call(
        kernel,
        out_shape=[jax.ShapeDtypeStruct(shape, dtype) for shape, dtype in outs],
        in_specs=[pl.BlockSpec(memory_space=pltpu.SMEM)]
        + [pl.BlockSpec(memory_space=pltpu.VMEM)] * len(args),
        out_specs=[pl.BlockSpec(memory_space=pltpu.VMEM)] * len(outs),
        scratch_shapes=scratch,
        compiler_params=pltpu.CompilerParams(vmem_limit_bytes=VMEM_LIMIT),
        cost_estimate=pl.CostEstimate(flops=0, bytes_accessed=0, transcendentals=0),
    )(place.reshape(1), *args)


def pack(arrays, place):
    rows, width = arrays[0].shape[-2], arrays[0].shape[-1] // GROUP
    counts = [1 if value.ndim == 2 else value.shape[0] for value in arrays]
    total = sum(counts)

    def kernel(at, *refs):
        chunks = refs[-1]
        i = 0
        for ref, count in zip(refs, counts):
            for j in range(count):
                for s in range(GROUP):
                    columns = slice(s * width, (s + 1) * width)
                    value = ref[:, columns] if len(ref.shape) == 2 else ref[j, :, columns]
                    chunks[s, :, i * width : (i + 1) * width] = value
                i += 1
        for d in range(GROUP):
            refs[len(arrays) + d][...] = chunks[at[0] ^ d]

    shape = (rows, total * width)
    return place_call(
        kernel,
        [(shape, bf16)] * GROUP,
        arrays,
        place,
        pltpu.VMEM((GROUP,) + shape, bf16),
    )


def join(parts, place):
    def kernel(at, *refs):
        for d in range(GROUP):
            refs[GROUP][at[0] ^ d] = refs[d][...]

    rows, width = parts[0].shape
    joined = place_call(kernel, [((GROUP, rows, width), bf16)], parts, place)[0]
    return joined.reshape(GROUP * rows, width)


def unpack(parts, counts, place):
    rows, width = parts[0].shape
    width = width // sum(counts)

    def kernel(at, *refs):
        chunks = refs[-1]
        for d in range(GROUP):
            chunks[at[0] ^ d] = refs[d][...].astype(f32)
        i = 0
        for ref, count in zip(refs[GROUP:], counts):
            for j in range(count):
                for s in range(GROUP):
                    columns = slice(s * width, (s + 1) * width)
                    ref[j, :, columns] = chunks[s, :, i * width : (i + 1) * width]
                i += 1

    return place_call(
        kernel,
        [((count, rows, GROUP * width), f32) for count in counts],
        parts,
        place,
        pltpu.VMEM((GROUP, rows, sum(counts) * width), f32),
    )


def collect_rows(pieces, dp, width):
    steps, _, columns = pieces[0].shape

    def kernel(at, *refs):
        blocks, flat = refs[-2], refs[-1]
        for d in range(GROUP):
            for m in range(steps):
                rows = [refs[d][m, i ^ d : (i ^ d) + 1, :] for i in (0, 2, 1, 3)]
                blocks[at[0] ^ (m * GROUP + d)] = jnp.concatenate(rows, axis=0)
        for k in range(steps * GROUP):
            flat[:, k * columns : (k + 1) * columns] = blocks[k]
        for i in range(6):
            refs[GROUP + i][...] = flat[:, i * width : (i + 1) * width]

    return place_call(
        kernel,
        [((GROUP, width), f32)] * 6,
        pieces,
        dp,
        pltpu.VMEM((steps * GROUP, GROUP, columns), f32),
        pltpu.VMEM((GROUP, 6 * width), f32),
    )


def deal_columns(own, other, dp, steps):
    width = own.shape[1]
    columns = 6 * width // (steps * GROUP)

    def kernel(at, a, b, out, blocks, flat):
        for i in range(6):
            flat[:, i * width : (i + 1) * width] = a[i : i + 1, :] + b[i : i + 1, :]
        for k in range(steps * GROUP):
            blocks[k] = flat[:, k * columns : (k + 1) * columns]
        for m in range(steps):
            for d in range(GROUP):
                out[m, d : d + 1, :] = blocks[at[0] ^ (m * GROUP + d)]

    return place_call(
        kernel,
        [((steps, GROUP, columns), f32)],
        (own, other),
        dp,
        pltpu.VMEM((steps * GROUP, 1, columns), f32),
        pltpu.VMEM((1, 6 * width), f32),
    )[0]


def split_four(value, place):
    rows = value.shape[0] // GROUP
    chunks = value.reshape(GROUP, rows, value.shape[1])

    def kernel(at, *refs):
        for d in range(GROUP):
            refs[1 + d][...] = refs[0][at[0] ^ d]

    return place_call(kernel, [((rows, value.shape[1]), bf16)] * GROUP, [chunks], place)


def row_sum(value):
    return jnp.sum(value, axis=0, keepdims=True)


def first_branch(parts, bias, inputs, gate, scale, shift):
    shape = inputs.shape

    def kernel(a, b, c, d, bi, x, g, sc, sh, branch_out, hidden_out, normed_out):
        branch = total_of((a, b, c, d)) + bi[...]
        hidden = x[...].astype(f32) + g[0:1, :] * branch
        branch_out[...] = branch
        hidden_out[...] = hidden
        normed_out[...] = (norm(hidden)[0] * (1.0 + sc[0:1, :]) + sh[0:1, :]).astype(bf16)

    return call(
        kernel,
        [(shape, f32), (shape, f32), (shape, bf16)],
        (*parts, bias, inputs, gate, scale, shift),
    )


def second_backward(parts, hidden, branch, cot, scale, gate):
    shape = hidden.shape

    def kernel(a, b, c, d, h, br, g, sc, gt, hidden_out, branch_out, sums):
        grad = total_of((a, b, c, d))
        normed, inverse = norm(h[...])
        grad_hidden = g[...].astype(f32) + norm_back(grad, normed, inverse, sc[0:1, :])
        hidden_out[...] = grad_hidden
        branch_out[...] = (gt[0:1, :] * grad_hidden).astype(bf16)
        sums[0:1, :] = row_sum(grad_hidden * br[...])
        sums[1:2, :] = row_sum(grad)
        sums[2:3, :] = row_sum(grad * normed)

    return call(
        kernel,
        [(shape, f32), (shape, bf16), ((3, shape[1]), f32)],
        (*parts, hidden, branch, cot, scale, gate),
    )


def second_branch(parts, bias, hidden, gate, cot):
    shape = hidden.shape

    def kernel(a, b, c, d, bi, h, gt, g, out, gate_sum):
        branch = total_of((a, b, c, d)) + bi[...]
        out[...] = (h[...] + gt[0:1, :] * branch).astype(bf16)
        gate_sum[...] = row_sum(g[...].astype(f32) * branch)

    return call(
        kernel, [(shape, bf16), ((1, shape[1]), f32)], (*parts, bias, hidden, gate, cot)
    )


def first_backward(parts, inputs, grad_hidden, scale, sums, gate_sum):
    shape = inputs.shape

    def kernel(a, b, c, d, x, gh, sc, s, gs, out, mod):
        grad = total_of((a, b, c, d))
        normed, inverse = norm(x[...].astype(f32))
        out[...] = (gh[...] + norm_back(grad, normed, inverse, sc[0:1, :])).astype(bf16)
        mod[0:1, :] = row_sum(grad)
        mod[1:2, :] = row_sum(grad * normed)
        mod[2:5, :] = s[...]
        mod[5:6, :] = gs[...]

    return call(
        kernel,
        [(shape, bf16), ((6, shape[1]), f32)],
        (*parts, inputs, grad_hidden, scale, sums, gate_sum),
    )


def head_masks(feats):
    lane = lax.broadcasted_iota(jnp.int32, (1, feats), 1)
    return [(lane >= h * HEAD) & (lane < (h + 1) * HEAD) for h in range(feats // HEAD)]


def only(mask, value):
    return jnp.where(mask, value, jnp.zeros_like(value))


def split_store(keep_ref, send_ref, value):
    half = value.shape[0] // 2
    keep_ref[...] = value[:half]
    send_ref[...] = value[half:].astype(bf16)


def attention_forward(near, far, shift, scale, weights, biases):
    total, width = 2 * near.shape[0], near.shape[1]
    feats = biases.shape[1]
    seq = total // GROUP
    factor = HEAD ** (-0.5)

    def kernel(t_near, t_far, sh, sc, w, b, normed, q_out, k_out, v_out, att, keep, send):
        for i in range(GROUP):
            rows = slice(i * seq, (i + 1) * seq)
            tok = t_near if i < GROUP // 2 else t_far
            value = norm(tok[i % 2 * seq : (i % 2 + 1) * seq, :].astype(f32))[0]
            normed[rows, :] = (value * (1.0 + sc[i : i + 1, :]) + sh[i : i + 1, :]).astype(bf16)
        projected = dot(normed[...], w[:, : 3 * feats])
        q_out[...] = (projected[:, :feats] + b[0:1, :]).astype(bf16)
        k_out[...] = projected[:, feats : 2 * feats].astype(bf16)
        v_out[...] = (projected[:, 2 * feats :] + b[1:2, :]).astype(bf16)
        masks = head_masks(feats)
        for i in range(GROUP):
            rows = slice(i * seq, (i + 1) * seq)
            q, k, v = q_out[rows, :], k_out[rows, :], v_out[rows, :]
            result = jnp.zeros((seq, feats), f32)
            for mask in masks:
                probs = softmax(dot_rows(only(mask, q), k) * factor)
                result += dot(probs.astype(bf16), only(mask, v))
            att[rows, :] = result.astype(bf16)
        split_store(keep, send, dot_rows(att[...], w[:, 3 * feats :]))

    return call(
        kernel,
        [
            ((total, width), bf16),
            ((total, feats), bf16),
            ((total, feats), bf16),
            ((total, feats), bf16),
            ((total, feats), bf16),
            ((total // 2, width), f32),
            ((total // 2, width), bf16),
        ],
        (near, far, shift, scale, weights, biases),
    )


def softmax(scores):
    exponent = jnp.exp(scores - jnp.max(scores, axis=-1, keepdims=True))
    return exponent / jnp.sum(exponent, axis=-1, keepdims=True)


def symmetric_sum(parts):
    pairs = [parts[2 * i] + parts[2 * i + 1] for i in range(GROUP)]
    return (pairs[0] + pairs[1]) + (pairs[2] + pairs[3])


def attention_backward(near, far, q_all, k_all, v_all, weights):
    total = q_all.shape[0]
    width, feats = weights.shape[0], q_all.shape[1]
    seq = total // GROUP
    factor = HEAD ** (-0.5)

    def kernel(g_near, g_far, q_in, k_in, v_in, w, grad_in, keep, send, bias, g, proj_bias):
        masks = head_masks(feats)
        g[: total // 2, :] = g_near[...]
        g[total // 2 :, :] = g_far[...]
        half = seq // 2
        proj_bias[...] = symmetric_sum(
            [row_sum(g[i * half : (i + 1) * half, :].astype(f32)) for i in range(2 * GROUP)]
        )
        grad_att = dot(g[...], w[:, 3 * feats :]).astype(bf16)
        q_sum = jnp.zeros((1, feats), f32)
        v_sum = jnp.zeros((1, feats), f32)
        for i in range(GROUP):
            rows = slice(i * seq, (i + 1) * seq)
            q, k, v = q_in[rows, :], k_in[rows, :], v_in[rows, :]
            ga = grad_att[rows, :]
            gq = jnp.zeros((seq, feats), f32)
            gk = jnp.zeros((seq, feats), f32)
            gv = jnp.zeros((seq, feats), f32)
            for mask in masks:
                probs = softmax(dot_rows(only(mask, q), k) * factor)
                gv += only(mask, transposed_dot(probs.astype(bf16), ga))
                gp = dot_rows(only(mask, ga), v)
                gs = probs * (gp - jnp.sum(probs * gp, axis=-1, keepdims=True))
                gs = gs.astype(bf16)
                gq += only(mask, dot(gs, k))
                gk += only(mask, transposed_dot(gs, q))
            gq, gk = gq * factor, gk * factor
            q_sum += jnp.sum(gq, axis=0, keepdims=True)
            v_sum += jnp.sum(gv, axis=0, keepdims=True)
            grad_in[rows, :] = jnp.concatenate([gq, gk, gv], axis=1).astype(bf16)
        bias[0:1, :] = q_sum
        bias[1:2, :] = v_sum
        split_store(keep, send, dot_rows(grad_in[...], w[:, : 3 * feats]))

    return call(
        kernel,
        [
            ((total, 3 * feats), bf16),
            ((total // 2, width), f32),
            ((total // 2, width), bf16),
            ((2, feats), f32),
            ((total, width), bf16),
            ((1, width), f32),
        ],
        (near, far, q_all, k_all, v_all, weights),
    )


def attention_weights(grad_in, normed, grad_branch, att):
    width, feats = normed.shape[1], att.shape[1]

    def kernel(gi, n, g, a, grads):
        grads[:, : 3 * feats] = transposed_dot(n[...], gi[...]).astype(bf16)
        grads[:, 3 * feats :] = transposed_dot(g[...], a[...]).astype(bf16)

    return call(kernel, [((width, 4 * feats), bf16)], (grad_in, normed, grad_branch, att))[0]


def feed_forward(near, far, weights, bias, cot_near, cot_far, gate):
    total, width = 2 * near.shape[0], near.shape[1]
    units = weights.shape[1] // 2
    seq = total // GROUP

    def kernel(
        n_near, n_far, w, b, c_near, c_far, gt, grads, keep, send, act_out, bias_out, fc2_out, grad_out, n
    ):
        n[: total // 2, :] = n_near[...]
        n[total // 2 :, :] = n_far[...]
        sums = []
        half = seq // 2
        for i in range(2 * GROUP):
            c = c_near if i < GROUP else c_far
            value = c[i % GROUP * half : (i % GROUP + 1) * half, :].astype(f32)
            value = value * gt[i // 2 : i // 2 + 1, :]
            sums.append(row_sum(value))
            grad_out[i * half : (i + 1) * half, :] = value.astype(bf16)
        fc2_out[...] = symmetric_sum(sums)
        pre = dot(n[...], w[:, :units]) + b[...]
        inner = ROOT * (pre + 0.044715 * (pre * pre * pre))
        tanh = jnp.tanh(inner)
        act = (0.5 * pre * (1.0 + tanh)).astype(bf16)
        slope = 0.5 * (1.0 + tanh) + 0.5 * pre * (1.0 - tanh * tanh) * (
            ROOT * (1.0 + 3 * 0.044715 * (pre * pre))
        )
        grad_pre = dot(grad_out[...], w[:, units:]) * slope
        bias_out[...] = jnp.sum(grad_pre, axis=0, keepdims=True)
        grad_pre = grad_pre.astype(bf16)
        grads[:, units:] = transposed_dot(grad_out[...], act).astype(bf16)
        grads[:, :units] = transposed_dot(n[...], grad_pre).astype(bf16)
        split_store(keep, send, dot_rows(grad_pre, w[:, :units]))
        act_out[...] = act

    return call(
        kernel,
        [
            ((width, 2 * units), bf16),
            ((total // 2, width), f32),
            ((total // 2, width), bf16),
            ((total, units), bf16),
            ((1, units), f32),
            ((1, width), f32),
            ((total, width), bf16),
            ((total, width), bf16),
        ],
        (near, far, weights, bias, cot_near, cot_far, gate),
    )


def feed_forward_out(act, weights):
    total, units = act.shape
    width = weights.shape[0]

    def kernel(a, w, keep, send):
        split_store(keep, send, dot_rows(a[...], w[:, units:]))

    return call(
        kernel,
        [((total // 2, width), f32), ((total // 2, width), bf16)],
        (act, weights),
    )


def local(
    tokens,
    conditions,
    mod_weight,
    mod_bias,
    qkv_weight,
    qv_bias,
    proj_weight,
    proj_bias,
    fc1_weight,
    fc1_bias,
    fc2_weight,
    fc2_bias,
    cotangent,
):
    seq, width = tokens.shape
    rows = seq // 2
    d_rows = qkv_weight.shape[0]
    t_width = qkv_weight.shape[2]
    hidden = fc1_weight.shape[1]
    feats = t_width // GROUP
    units = hidden // GROUP
    n_dp = width // d_rows
    t = lax.axis_index("tensor")
    place = lax.axis_index("xx") * 2 + lax.axis_index("core")
    dp = lax.axis_index("zz") * GROUP + place

    attn_arrays = [qkv_weight.transpose(1, 0, 2), proj_weight.T]
    attn_part = join(send_four(pack(attn_arrays, place)), place)
    attn_full = lax.all_gather(attn_part, "zz", axis=0, tiled=True)

    cond_values = after(conditions, attn_part).astype(f32)
    silu_conds = jax.nn.silu(cond_values).astype(bf16)
    small = jnp.concatenate(
        [silu_conds, qv_bias, proj_bias[None], fc1_bias, fc2_bias[None]], axis=1
    )
    small = gather_dp(small)
    all_silu = small[:, :width]
    spots = jnp.arange(n_dp)
    order = ((spots[:, None] ^ dp) == spots[None]).astype(bf16)
    biases = product(order, small[:, width:], "ij,jc->ic")
    n_qv, n_b, n_f = qv_bias.shape[1], proj_bias.shape[0], fc1_bias.shape[1]
    cuts = [n_qv, n_qv + n_b, n_qv + n_b + n_f]
    qv_full = biases[:, : cuts[0]].reshape(2, GROUP, feats)
    proj_bias_full = biases[:, cuts[0] : cuts[1]].reshape(width)
    fc1_bias_full = biases[:, cuts[1] : cuts[2]].reshape(GROUP, units)
    fc2_bias_full = biases[:, cuts[2] :].reshape(width)
    qv_here = lax.dynamic_index_in_dim(qv_full, place, 1, keepdims=False)
    fc1_bias_here = lax.dynamic_index_in_dim(fc1_bias_full, place, 0, keepdims=False)
    mod_columns = product(all_silu, mod_weight, "ld,dc->lc") + mod_bias.astype(f32)
    n_zz = n_dp // GROUP
    mod_parts = send_zz([mod_columns[m * GROUP : (m + 1) * GROUP] for m in range(n_zz)])
    mod_parts = after(jnp.stack(mod_parts), attn_full)
    mod_parts = send_four([mod_parts] * GROUP)
    modulation = collect_rows(mod_parts, dp, width)
    shift_attn, scale_attn, gate_attn, shift_mlp, scale_mlp, gate_mlp = modulation
    mlp_arrays = [after(fc1_weight, mod_columns), fc2_weight.T]
    mlp_part = join(send_four(pack(mlp_arrays, place)), place)
    mlp_full = lax.all_gather(mlp_part, "zz", axis=0, tiled=True)
    def own_order(value):
        first = lax.dynamic_slice_in_dim(value, t * rows, rows, 0)
        second = lax.dynamic_slice_in_dim(value, (1 - t) * rows, rows, 0)
        return jnp.concatenate([first, second], axis=0)

    def true_order(own, other):
        return jnp.where(
            t == 0,
            jnp.concatenate([own, other], axis=0),
            jnp.concatenate([other, own], axis=0),
        )

    tokens_own = own_order(tokens)
    cot_own = own_order(after(cotangent, mod_columns))
    tokens_near, tokens_far = gather_four(tokens_own)
    cot_near, cot_far = gather_four(cot_own)
    inputs_half = tokens_own[:rows]
    grad_out_half = cot_own[:rows]

    normed_one, queries, keys, values, attended, keep, send = attention_forward(
        tokens_near, tokens_far, shift_attn, scale_attn, attn_full, qv_here
    )
    branch_half, hidden_half, normed_two_half = first_branch(
        scatter_eight(keep, send),
        proj_bias_full[None],
        inputs_half,
        gate_attn,
        scale_mlp,
        shift_mlp,
    )

    normed_two_half = after(normed_two_half, cot_far)
    near, far = gather_eight(normed_two_half, mlp_full)
    mlp_grad, keep, send, activated, fc1_bias_part, fc2_bias_part, _, _ = feed_forward(
        near, far, mlp_full, fc1_bias_here[None], cot_near, cot_far, gate_mlp
    )
    mlp_grad = lax.psum_scatter(mlp_grad, "zz", scatter_dimension=0, tiled=True)
    grad_hidden_half, grad_branch_half, mod_sums = second_backward(
        scatter_eight(keep, send), hidden_half, branch_half, grad_out_half, scale_mlp, gate_attn
    )
    near, far = gather_eight(grad_branch_half)

    grad_in, keep, send, qv_bias_part, grad_branch_all, proj_bias_part = attention_backward(
        near, far, queries, keys, values, attn_full
    )

    out_keep, out_send = feed_forward_out(after(activated, grad_branch_half), mlp_full)
    block_half, gate_sum = second_branch(
        scatter_eight(out_keep, out_send),
        fc2_bias_full[None],
        hidden_half,
        gate_mlp,
        grad_out_half,
    )

    biases = jnp.concatenate(
        [
            qv_bias_part.reshape(-1),
            fc1_bias_part[0],
            proj_bias_part[0],
            fc2_bias_part[0],
        ]
    )
    biases = sum(send_zz([after(biases, gate_sum)] * n_zz))
    own = 2 * feats + units
    group_biases = jnp.concatenate(send_four([biases[None, :own]] * GROUP), axis=0)
    group_biases = reorder(group_biases, place)
    qv_all = jnp.concatenate(
        [group_biases[:, :feats].reshape(-1), group_biases[:, feats : 2 * feats].reshape(-1)]
    )
    fc1_all = group_biases[:, 2 * feats :].reshape(-1)
    proj_all = biases[own : own + width]
    fc2_all = biases[own + width :]

    attn_grads = attention_weights(
        after(grad_in, mlp_grad, biases, group_biases),
        normed_one,
        grad_branch_all,
        attended,
    )
    attn_grad = lax.psum_scatter(attn_grads, "zz", scatter_dimension=0, tiled=True)
    tokens_grad_half, grad_mod = first_backward(
        scatter_eight(keep, after(send, attn_grads)),
        inputs_half,
        grad_hidden_half,
        scale_attn,
        mod_sums,
        gate_sum,
    )

    block_out = true_order(block_half, exchange(block_half, "tensor"))
    tokens_grad = true_order(tokens_grad_half, exchange(tokens_grad_half, "tensor")).astype(f32)
    mlp_parts = send_four(split_four(mlp_grad, place))
    fc1_weight_grad, fc2_weight_grad = unpack(mlp_parts, (1, 1), place)
    grad_mod_other = exchange(after(grad_mod, fc1_weight_grad), "tensor")
    dealt = deal_columns(grad_mod, grad_mod_other, dp, n_zz)
    dealt = jnp.stack(send_zz([dealt[m] for m in range(n_zz)]))
    attn_parts = split_four(after(attn_grad, fc1_weight_grad), place)
    dealt = jnp.stack(send_four([dealt[:, d] for d in range(GROUP)]), axis=1)
    grad_mod_columns = dealt.reshape(n_dp, dealt.shape[2]).astype(bf16)
    mod_bias_grad = jnp.sum(grad_mod_columns.astype(f32), axis=0)
    mod_weight_grad = product(all_silu, grad_mod_columns, "ld,lc->dc")
    late_columns = after(grad_mod_columns, attn_parts[0])
    grad_silu = product(late_columns, mod_weight, "lc,dc->ld")
    attn_parts = send_four(attn_parts)
    grad_silu = scatter_dp(grad_silu, *attn_parts)
    conditions_grad = jax.vjp(jax.nn.silu, cond_values)[1](grad_silu)[0]

    def piece(vector):
        size = vector.shape[0] // n_dp
        return lax.dynamic_slice_in_dim(vector, dp * size, size, 0)

    qkv_weight_grad, proj_weight_grad = unpack(attn_parts, (3, 1), place)
    qkv_weight_grad = qkv_weight_grad.transpose(1, 0, 2)
    fc1_weight_grad = fc1_weight_grad[0]
    fc2_weight_grad = fc2_weight_grad[0].T
    proj_weight_grad = proj_weight_grad[0].T
    return (
        block_out,
        tokens_grad,
        conditions_grad,
        mod_weight_grad,
        mod_bias_grad,
        qkv_weight_grad,
        piece(qv_all)[None],
        proj_weight_grad,
        piece(proj_all),
        fc1_weight_grad,
        piece(fc1_all)[None],
        fc2_weight_grad,
        piece(fc2_all),
    )


def solution(mesh):
    n_dp, n_tensor = mesh.shape["dp"], mesh.shape["tensor"]
    cut = Mesh(
        mesh.devices.reshape(n_dp // GROUP, 2, 2, n_tensor), ("zz", "xx", "core", "tensor")
    )
    dp = ("zz", "xx", "core")
    return jax.shard_map(
        local,
        mesh=cut,
        in_specs=(
            P(dp, None),
            P(dp, None),
            P(None, dp),
            P(dp),
            P(dp, None, "tensor"),
            P("tensor", dp),
            P("tensor", dp),
            P(dp),
            P(dp, "tensor"),
            P("tensor", dp),
            P("tensor", dp),
            P(dp),
            P(dp, None),
        ),
        out_specs=(
            P(dp, None),
            P(dp, None),
            P(dp, None),
            P(None, dp),
            P(dp),
            P(dp, None, "tensor"),
            P("tensor", dp),
            P("tensor", dp),
            P(dp),
            P(dp, "tensor"),
            P("tensor", dp),
            P("tensor", dp),
            P(dp),
        ),
        check_vma=False,
    )
```

```python
import jax
import jax.numpy as jnp
from jax import lax
from jax.experimental import pallas as pl
from jax.experimental.pallas import tpu as pltpu
from jax.sharding import Mesh, PartitionSpec as P

HEAD = 72
EPSILON = 1e-06
GROUP = 4
ROOT = 0.7978845608028654
VMEM_LIMIT = 48 * 1024 * 1024

bf16 = jnp.bfloat16
f32 = jnp.float32


def product(left, right, form):
    return jnp.einsum(form, left, right, preferred_element_type=f32)


def exchange(value, axis, mask=1):
    size = lax.axis_size(axis)
    return lax.ppermute(value, axis, [(i, i ^ mask) for i in range(size)])


def reorder(value, position):
    count = value.shape[0]
    bit = 1
    while bit < count:
        parts = value.reshape((count // (2 * bit), 2, bit) + value.shape[1:])
        flip = (position // bit) % 2 == 1
        first = jnp.where(flip, parts[:, 1], parts[:, 0])
        second = jnp.where(flip, parts[:, 0], parts[:, 1])
        value = jnp.stack([first, second], axis=1).reshape(value.shape)
        bit *= 2
    return value


def after(value, *others):
    def nothing(*refs):
        pass

    return pl.pallas_call(
        nothing,
        out_shape=jax.ShapeDtypeStruct(value.shape, value.dtype),
        in_specs=[pl.BlockSpec(memory_space=pl.ANY)] * (1 + len(others)),
        out_specs=pl.BlockSpec(memory_space=pl.ANY),
        input_output_aliases={0: 0},
    )(value, *others)


def send_four(parts):
    return [
        parts[0],
        exchange(parts[1], "core"),
        exchange(parts[2], "xx"),
        exchange(parts[3], ("xx", "core"), 3),
    ]


def send_zz(parts):
    return [parts[0]] + [exchange(parts[m], "zz", m) for m in range(1, len(parts))]


def gather_dp(value):
    four = jnp.concatenate(send_four([value] * GROUP), axis=0)
    return jnp.concatenate(send_zz([four] * lax.axis_size("zz")), axis=0)


def scatter_dp(value, *others):
    steps = lax.axis_size("zz")
    four = sum(send_zz([value[m * GROUP : (m + 1) * GROUP] for m in range(steps)]))
    four = after(four, *others)
    return sum(send_four([four[d : d + 1] for d in range(GROUP)]))


def gather_four(value):
    near = jnp.concatenate([value, exchange(value, "xx")], axis=0)
    return near, exchange(near, "core")


def gather_eight(value, *others):
    parts = send_plane([value] * 4)

    def kernel(*refs):
        rows = value.shape[0]
        for i in range(4):
            refs[4][i * rows : (i + 1) * rows, :] = refs[i][...]

    near = call(kernel, [((4 * value.shape[0], value.shape[1]), bf16)], parts)[0]
    if others:
        near = after(near, *others)
    return near, exchange(near, "core")


def send_plane(parts):
    return [
        parts[0],
        exchange(parts[1], "tensor"),
        exchange(parts[2], "xx"),
        exchange(parts[3], ("xx", "tensor"), 3),
    ]


def scatter_eight(keep, send):
    rows = keep.shape[0] // 4
    shape = (rows, keep.shape[1])

    def kernel(a, b, own, *sent):
        own[...] = a[:rows, :] + b[:rows, :].astype(f32)
        for i in range(1, 4):
            part = slice(i * rows, (i + 1) * rows)
            sent[i - 1][...] = (a[part, :] + b[part, :].astype(f32)).astype(bf16)

    got = exchange(send, "core")
    return send_plane(call(kernel, [(shape, f32)] + [(shape, bf16)] * 3, (keep, got)))


def total_of(refs):
    own, one, two, three = [ref[...].astype(f32) for ref in refs]
    return (own + one) + (two + three)


def norm(values):
    mean = jnp.mean(values, axis=-1, keepdims=True)
    centered = values - mean
    variance = jnp.mean(centered * centered, axis=-1, keepdims=True)
    inverse = lax.rsqrt(variance + EPSILON)
    return centered * inverse, inverse


def norm_back(grad, normed, inverse, scale):
    scaled = grad * (1.0 + scale)
    mean_scaled = jnp.mean(scaled, axis=-1, keepdims=True)
    mean_product = jnp.mean(scaled * normed, axis=-1, keepdims=True)
    return inverse * (scaled - mean_scaled - normed * mean_product)


def transposed_dot(left, right):
    return lax.dot_general(left, right, (((0,), (0,)), ((), ())), preferred_element_type=f32)


def dot_rows(left, right):
    return lax.dot_general(left, right, (((1,), (1,)), ((), ())), preferred_element_type=f32)


def dot(left, right):
    return lax.dot_general(left, right, (((1,), (0,)), ((), ())), preferred_element_type=f32)


def call(kernel, outs, args, flops=0):
    return pl.pallas_call(
        kernel,
        out_shape=[jax.ShapeDtypeStruct(shape, dtype) for shape, dtype in outs],
        in_specs=[pl.BlockSpec(memory_space=pltpu.VMEM)] * len(args),
        out_specs=[pl.BlockSpec(memory_space=pltpu.VMEM)] * len(outs),
        compiler_params=pltpu.CompilerParams(vmem_limit_bytes=VMEM_LIMIT),
        cost_estimate=pl.CostEstimate(flops=flops, bytes_accessed=0, transcendentals=0),
    )(*args)


def place_call(kernel, outs, args, place, *scratch):
    return pl.pallas_call(
        kernel,
        out_shape=[jax.ShapeDtypeStruct(shape, dtype) for shape, dtype in outs],
        in_specs=[pl.BlockSpec(memory_space=pltpu.SMEM)]
        + [pl.BlockSpec(memory_space=pltpu.VMEM)] * len(args),
        out_specs=[pl.BlockSpec(memory_space=pltpu.VMEM)] * len(outs),
        scratch_shapes=scratch,
        compiler_params=pltpu.CompilerParams(vmem_limit_bytes=VMEM_LIMIT),
        cost_estimate=pl.CostEstimate(flops=0, bytes_accessed=0, transcendentals=0),
    )(place.reshape(1), *args)


def pack(arrays, place):
    rows, width = arrays[0].shape[-2], arrays[0].shape[-1] // GROUP
    counts = [1 if value.ndim == 2 else value.shape[0] for value in arrays]
    total = sum(counts)

    def kernel(at, *refs):
        chunks = refs[-1]
        i = 0
        for ref, count in zip(refs, counts):
            for j in range(count):
                for s in range(GROUP):
                    columns = slice(s * width, (s + 1) * width)
                    value = ref[:, columns] if len(ref.shape) == 2 else ref[j, :, columns]
                    chunks[s, :, i * width : (i + 1) * width] = value
                i += 1
        for d in range(GROUP):
            refs[len(arrays) + d][...] = chunks[at[0] ^ d]

    shape = (rows, total * width)
    return place_call(
        kernel,
        [(shape, bf16)] * GROUP,
        arrays,
        place,
        pltpu.VMEM((GROUP,) + shape, bf16),
    )


def join(parts, place):
    def kernel(at, *refs):
        for d in range(GROUP):
            refs[GROUP][at[0] ^ d] = refs[d][...]

    rows, width = parts[0].shape
    joined = place_call(kernel, [((GROUP, rows, width), bf16)], parts, place)[0]
    return joined.reshape(GROUP * rows, width)


def unpack(parts, counts, place):
    rows, width = parts[0].shape
    width = width // sum(counts)

    def kernel(at, *refs):
        chunks = refs[-1]
        for d in range(GROUP):
            chunks[at[0] ^ d] = refs[d][...].astype(f32)
        i = 0
        for ref, count in zip(refs[GROUP:], counts):
            for j in range(count):
                for s in range(GROUP):
                    columns = slice(s * width, (s + 1) * width)
                    ref[j, :, columns] = chunks[s, :, i * width : (i + 1) * width]
                i += 1

    return place_call(
        kernel,
        [((count, rows, GROUP * width), f32) for count in counts],
        parts,
        place,
        pltpu.VMEM((GROUP, rows, sum(counts) * width), f32),
    )


def collect_rows(pieces, dp, width):
    steps, _, columns = pieces[0].shape

    def kernel(at, *refs):
        blocks, flat = refs[-2], refs[-1]
        for d in range(GROUP):
            for m in range(steps):
                rows = [refs[d][m, i ^ d : (i ^ d) + 1, :] for i in (0, 2, 1, 3)]
                blocks[at[0] ^ (m * GROUP + d)] = jnp.concatenate(rows, axis=0)
        for k in range(steps * GROUP):
            flat[:, k * columns : (k + 1) * columns] = blocks[k]
        for i in range(6):
            refs[GROUP + i][...] = flat[:, i * width : (i + 1) * width]

    return place_call(
        kernel,
        [((GROUP, width), f32)] * 6,
        pieces,
        dp,
        pltpu.VMEM((steps * GROUP, GROUP, columns), f32),
        pltpu.VMEM((GROUP, 6 * width), f32),
    )


def deal_columns(own, other, biases, dp, steps):
    width = own.shape[1]
    columns = 6 * width // (steps * GROUP)
    extra = -(-sum(value.size for value in biases) // columns)

    def kernel(at, a, b, *refs):
        out, blocks, flat, flat_bias = refs[-4:]
        for i in range(6):
            flat[:, i * width : (i + 1) * width] = a[i : i + 1, :] + b[i : i + 1, :]
        for k in range(steps * GROUP):
            blocks[k] = flat[:, k * columns : (k + 1) * columns]
        flat_bias[...] = jnp.zeros_like(flat_bias)
        start = 0
        for ref in refs[: len(biases)]:
            for i in range(ref.shape[0]):
                flat_bias[:, start : start + ref.shape[1]] = ref[i : i + 1, :]
                start += ref.shape[1]
        for m in range(steps):
            for d in range(GROUP):
                out[m, d : d + 1, :] = blocks[at[0] ^ (m * GROUP + d)]
            for r in range(extra):
                part = flat_bias[:, r * columns : (r + 1) * columns]
                out[m, GROUP + r : GROUP + r + 1, :] = part

    return place_call(
        kernel,
        [((steps, GROUP + extra, columns), f32)],
        (own, other, *biases),
        dp,
        pltpu.VMEM((steps * GROUP, 1, columns), f32),
        pltpu.VMEM((1, 6 * width), f32),
        pltpu.VMEM((1, extra * columns), f32),
    )[0]


def deal_again(pieces, count):
    steps = len(pieces)
    columns = pieces[0].shape[1]
    extra = pieces[0].shape[0] - GROUP

    def kernel(*refs):
        sums = refs[0][GROUP:, :]
        for m in range(1, steps):
            sums = sums + refs[m][GROUP:, :]
        refs[-1][...] = sums
        for d in range(GROUP):
            out = refs[steps + d]
            for m in range(steps):
                out[m : m + 1, :] = refs[m][d : d + 1, :]
            out[steps:, :] = sums[:count, :]

    outs = call(
        kernel,
        [((steps + count, columns), f32)] * GROUP + [((extra, columns), f32)],
        pieces,
    )
    return outs[:GROUP], outs[GROUP]


def split_four(value, place):
    rows = value.shape[0] // GROUP
    chunks = value.reshape(GROUP, rows, value.shape[1])

    def kernel(at, *refs):
        for d in range(GROUP):
            refs[1 + d][...] = refs[0][at[0] ^ d]

    return place_call(kernel, [((rows, value.shape[1]), bf16)] * GROUP, [chunks], place)


def row_sum(value):
    return jnp.sum(value, axis=0, keepdims=True)


def first_branch(parts, bias, inputs, gate, scale, shift):
    shape = inputs.shape

    def kernel(a, b, c, d, bi, x, g, sc, sh, branch_out, hidden_out, normed_out):
        branch = total_of((a, b, c, d)) + bi[...]
        hidden = x[...].astype(f32) + g[0:1, :] * branch
        branch_out[...] = branch
        hidden_out[...] = hidden
        normed_out[...] = (norm(hidden)[0] * (1.0 + sc[0:1, :]) + sh[0:1, :]).astype(bf16)

    return call(
        kernel,
        [(shape, f32), (shape, f32), (shape, bf16)],
        (*parts, bias, inputs, gate, scale, shift),
    )


def second_backward(parts, hidden, branch, cot, scale, gate):
    shape = hidden.shape

    def kernel(a, b, c, d, h, br, g, sc, gt, hidden_out, branch_out, sums):
        grad = total_of((a, b, c, d))
        normed, inverse = norm(h[...])
        grad_hidden = g[...].astype(f32) + norm_back(grad, normed, inverse, sc[0:1, :])
        hidden_out[...] = grad_hidden
        branch_out[...] = (gt[0:1, :] * grad_hidden).astype(bf16)
        sums[0:1, :] = row_sum(grad_hidden * br[...])
        sums[1:2, :] = row_sum(grad)
        sums[2:3, :] = row_sum(grad * normed)

    return call(
        kernel,
        [(shape, f32), (shape, bf16), ((3, shape[1]), f32)],
        (*parts, hidden, branch, cot, scale, gate),
    )


def second_branch(parts, bias, hidden, gate, cot):
    shape = hidden.shape

    def kernel(a, b, c, d, bi, h, gt, g, out, gate_sum):
        branch = total_of((a, b, c, d)) + bi[...]
        out[...] = (h[...] + gt[0:1, :] * branch).astype(bf16)
        gate_sum[...] = row_sum(g[...].astype(f32) * branch)

    return call(
        kernel, [(shape, bf16), ((1, shape[1]), f32)], (*parts, bias, hidden, gate, cot)
    )


def first_backward(parts, inputs, grad_hidden, scale, sums, gate_sum):
    shape = inputs.shape

    def kernel(a, b, c, d, x, gh, sc, s, gs, out, mod):
        grad = total_of((a, b, c, d))
        normed, inverse = norm(x[...].astype(f32))
        out[...] = (gh[...] + norm_back(grad, normed, inverse, sc[0:1, :])).astype(bf16)
        mod[0:1, :] = row_sum(grad)
        mod[1:2, :] = row_sum(grad * normed)
        mod[2:5, :] = s[...]
        mod[5:6, :] = gs[...]

    return call(
        kernel,
        [(shape, bf16), ((6, shape[1]), f32)],
        (*parts, inputs, grad_hidden, scale, sums, gate_sum),
    )


def head_masks(feats):
    lane = lax.broadcasted_iota(jnp.int32, (1, feats), 1)
    return [(lane >= h * HEAD) & (lane < (h + 1) * HEAD) for h in range(feats // HEAD)]


def only(mask, value):
    return jnp.where(mask, value, jnp.zeros_like(value))


def split_store(keep_ref, send_ref, value):
    half = value.shape[0] // 2
    keep_ref[...] = value[:half]
    send_ref[...] = value[half:].astype(bf16)


def attention_forward(near, far, shift, scale, weights, biases):
    total, width = 2 * near.shape[0], near.shape[1]
    feats = biases.shape[1]
    seq = total // GROUP
    factor = HEAD ** (-0.5)

    def kernel(t_near, t_far, sh, sc, w, b, normed, q_out, k_out, v_out, att, keep, send):
        for i in range(GROUP):
            rows = slice(i * seq, (i + 1) * seq)
            tok = t_near if i < GROUP // 2 else t_far
            value = norm(tok[i % 2 * seq : (i % 2 + 1) * seq, :].astype(f32))[0]
            normed[rows, :] = (value * (1.0 + sc[i : i + 1, :]) + sh[i : i + 1, :]).astype(bf16)
        projected = dot(normed[...], w[:, : 3 * feats])
        q_out[...] = (projected[:, :feats] + b[0:1, :]).astype(bf16)
        k_out[...] = projected[:, feats : 2 * feats].astype(bf16)
        v_out[...] = (projected[:, 2 * feats :] + b[1:2, :]).astype(bf16)
        masks = head_masks(feats)
        for i in range(GROUP):
            rows = slice(i * seq, (i + 1) * seq)
            q, k, v = q_out[rows, :], k_out[rows, :], v_out[rows, :]
            result = jnp.zeros((seq, feats), f32)
            for mask in masks:
                probs = softmax(dot_rows(only(mask, q), k) * factor)
                result += dot(probs.astype(bf16), only(mask, v))
            att[rows, :] = result.astype(bf16)
        split_store(keep, send, dot_rows(att[...], w[:, 3 * feats :]))

    return call(
        kernel,
        [
            ((total, width), bf16),
            ((total, feats), bf16),
            ((total, feats), bf16),
            ((total, feats), bf16),
            ((total, feats), bf16),
            ((total // 2, width), f32),
            ((total // 2, width), bf16),
        ],
        (near, far, shift, scale, weights, biases),
    )


def softmax(scores):
    exponent = jnp.exp(scores - jnp.max(scores, axis=-1, keepdims=True))
    return exponent / jnp.sum(exponent, axis=-1, keepdims=True)


def symmetric_sum(parts):
    pairs = [parts[2 * i] + parts[2 * i + 1] for i in range(GROUP)]
    return (pairs[0] + pairs[1]) + (pairs[2] + pairs[3])


def attention_backward(near, far, q_all, k_all, v_all, weights):
    total = q_all.shape[0]
    width, feats = weights.shape[0], q_all.shape[1]
    seq = total // GROUP
    factor = HEAD ** (-0.5)

    def kernel(g_near, g_far, q_in, k_in, v_in, w, grad_in, keep, send, bias, g, proj_bias):
        masks = head_masks(feats)
        g[: total // 2, :] = g_near[...]
        g[total // 2 :, :] = g_far[...]
        half = seq // 2
        proj_bias[...] = symmetric_sum(
            [row_sum(g[i * half : (i + 1) * half, :].astype(f32)) for i in range(2 * GROUP)]
        )
        grad_att = dot(g[...], w[:, 3 * feats :]).astype(bf16)
        q_sum = jnp.zeros((1, feats), f32)
        v_sum = jnp.zeros((1, feats), f32)
        for i in range(GROUP):
            rows = slice(i * seq, (i + 1) * seq)
            q, k, v = q_in[rows, :], k_in[rows, :], v_in[rows, :]
            ga = grad_att[rows, :]
            gq = jnp.zeros((seq, feats), f32)
            gk = jnp.zeros((seq, feats), f32)
            gv = jnp.zeros((seq, feats), f32)
            for mask in masks:
                probs = softmax(dot_rows(only(mask, q), k) * factor)
                gv += only(mask, transposed_dot(probs.astype(bf16), ga))
                gp = dot_rows(only(mask, ga), v)
                gs = probs * (gp - jnp.sum(probs * gp, axis=-1, keepdims=True))
                gs = gs.astype(bf16)
                gq += only(mask, dot(gs, k))
                gk += only(mask, transposed_dot(gs, q))
            gq, gk = gq * factor, gk * factor
            q_sum += jnp.sum(gq, axis=0, keepdims=True)
            v_sum += jnp.sum(gv, axis=0, keepdims=True)
            grad_in[rows, :] = jnp.concatenate([gq, gk, gv], axis=1).astype(bf16)
        bias[0:1, :] = q_sum
        bias[1:2, :] = v_sum
        split_store(keep, send, dot_rows(grad_in[...], w[:, : 3 * feats]))

    return call(
        kernel,
        [
            ((total, 3 * feats), bf16),
            ((total // 2, width), f32),
            ((total // 2, width), bf16),
            ((2, feats), f32),
            ((total, width), bf16),
            ((1, width), f32),
        ],
        (near, far, q_all, k_all, v_all, weights),
    )


def attention_weights(grad_in, normed, grad_branch, att):
    width, feats = normed.shape[1], att.shape[1]

    def kernel(gi, n, g, a, grads):
        grads[:, : 3 * feats] = transposed_dot(n[...], gi[...]).astype(bf16)
        grads[:, 3 * feats :] = transposed_dot(g[...], a[...]).astype(bf16)

    return call(kernel, [((width, 4 * feats), bf16)], (grad_in, normed, grad_branch, att))[0]


def feed_forward(near, far, weights, bias, cot_near, cot_far, gate):
    total, width = 2 * near.shape[0], near.shape[1]
    units = weights.shape[1] // 2
    seq = total // GROUP

    def kernel(
        n_near, n_far, w, b, c_near, c_far, gt, grads, keep, send, act_out, bias_out, fc2_out, grad_out, n
    ):
        n[: total // 2, :] = n_near[...]
        n[total // 2 :, :] = n_far[...]
        sums = []
        half = seq // 2
        for i in range(2 * GROUP):
            c = c_near if i < GROUP else c_far
            value = c[i % GROUP * half : (i % GROUP + 1) * half, :].astype(f32)
            value = value * gt[i // 2 : i // 2 + 1, :]
            sums.append(row_sum(value))
            grad_out[i * half : (i + 1) * half, :] = value.astype(bf16)
        fc2_out[...] = symmetric_sum(sums)
        pre = dot(n[...], w[:, :units]) + b[...]
        inner = ROOT * (pre + 0.044715 * (pre * pre * pre))
        tanh = jnp.tanh(inner)
        act = (0.5 * pre * (1.0 + tanh)).astype(bf16)
        slope = 0.5 * (1.0 + tanh) + 0.5 * pre * (1.0 - tanh * tanh) * (
            ROOT * (1.0 + 3 * 0.044715 * (pre * pre))
        )
        grad_pre = dot(grad_out[...], w[:, units:]) * slope
        bias_out[...] = jnp.sum(grad_pre, axis=0, keepdims=True)
        grad_pre = grad_pre.astype(bf16)
        grads[:, units:] = transposed_dot(grad_out[...], act).astype(bf16)
        grads[:, :units] = transposed_dot(n[...], grad_pre).astype(bf16)
        split_store(keep, send, dot_rows(grad_pre, w[:, :units]))
        act_out[...] = act

    return call(
        kernel,
        [
            ((width, 2 * units), bf16),
            ((total // 2, width), f32),
            ((total // 2, width), bf16),
            ((total, units), bf16),
            ((1, units), f32),
            ((1, width), f32),
            ((total, width), bf16),
            ((total, width), bf16),
        ],
        (near, far, weights, bias, cot_near, cot_far, gate),
    )


def feed_forward_out(act, weights):
    total, units = act.shape
    width = weights.shape[0]

    def kernel(a, w, keep, send):
        split_store(keep, send, dot_rows(a[...], w[:, units:]))

    return call(
        kernel,
        [((total // 2, width), f32), ((total // 2, width), bf16)],
        (act, weights),
    )


def local(
    tokens,
    conditions,
    mod_weight,
    mod_bias,
    qkv_weight,
    qv_bias,
    proj_weight,
    proj_bias,
    fc1_weight,
    fc1_bias,
    fc2_weight,
    fc2_bias,
    cotangent,
):
    seq, width = tokens.shape
    rows = seq // 2
    d_rows = qkv_weight.shape[0]
    t_width = qkv_weight.shape[2]
    hidden = fc1_weight.shape[1]
    feats = t_width // GROUP
    units = hidden // GROUP
    n_dp = width // d_rows
    t = lax.axis_index("tensor")
    place = lax.axis_index("xx") * 2 + lax.axis_index("core")
    dp = lax.axis_index("zz") * GROUP + place

    attn_arrays = [qkv_weight.transpose(1, 0, 2), proj_weight.T]
    attn_part = join(send_four(pack(attn_arrays, place)), place)
    attn_full = lax.all_gather(attn_part, "zz", axis=0, tiled=True)

    cond_values = conditions.astype(f32)
    silu_conds = jax.nn.silu(cond_values).astype(bf16)
    small = jnp.concatenate(
        [silu_conds, qv_bias, proj_bias[None], fc1_bias, fc2_bias[None]], axis=1
    )
    small = gather_dp(after(small, attn_part))
    all_silu = small[:, :width]
    spots = jnp.arange(n_dp)
    order = ((spots[:, None] ^ dp) == spots[None]).astype(bf16)
    biases = product(order, small[:, width:], "ij,jc->ic")
    n_qv, n_b, n_f = qv_bias.shape[1], proj_bias.shape[0], fc1_bias.shape[1]
    cuts = [n_qv, n_qv + n_b, n_qv + n_b + n_f]
    qv_full = biases[:, : cuts[0]].reshape(2, GROUP, feats)
    proj_bias_full = biases[:, cuts[0] : cuts[1]].reshape(width)
    fc1_bias_full = biases[:, cuts[1] : cuts[2]].reshape(GROUP, units)
    fc2_bias_full = biases[:, cuts[2] :].reshape(width)
    qv_here = lax.dynamic_index_in_dim(qv_full, place, 1, keepdims=False)
    fc1_bias_here = lax.dynamic_index_in_dim(fc1_bias_full, place, 0, keepdims=False)
    mod_columns = product(all_silu, mod_weight, "ld,dc->lc") + mod_bias.astype(f32)
    n_zz = n_dp // GROUP
    mod_parts = send_zz([mod_columns[m * GROUP : (m + 1) * GROUP] for m in range(n_zz)])
    mod_parts = after(jnp.stack(mod_parts), attn_full)
    mod_parts = send_four([mod_parts] * GROUP)
    modulation = collect_rows(mod_parts, dp, width)
    shift_attn, scale_attn, gate_attn, shift_mlp, scale_mlp, gate_mlp = modulation
    mlp_arrays = [fc1_weight, fc2_weight.T]
    mlp_part = join(send_four(pack(mlp_arrays, place)), place)
    mlp_full = lax.all_gather(mlp_part, "zz", axis=0, tiled=True)
    def own_order(value):
        first = lax.dynamic_slice_in_dim(value, t * rows, rows, 0)
        second = lax.dynamic_slice_in_dim(value, (1 - t) * rows, rows, 0)
        return jnp.concatenate([first, second], axis=0)

    def true_order(own, other):
        return jnp.where(
            t == 0,
            jnp.concatenate([own, other], axis=0),
            jnp.concatenate([other, own], axis=0),
        )

    tokens_own = own_order(tokens)
    cot_own = after(own_order(cotangent), mod_columns)
    tokens_near, tokens_far = gather_four(tokens_own)
    cot_near, cot_far = gather_four(cot_own)
    inputs_half = tokens_own[:rows]
    grad_out_half = cot_own[:rows]

    normed_one, queries, keys, values, attended, keep, send = attention_forward(
        tokens_near, tokens_far, shift_attn, scale_attn, attn_full, qv_here
    )
    branch_half, hidden_half, normed_two_half = first_branch(
        scatter_eight(keep, send),
        proj_bias_full[None],
        inputs_half,
        gate_attn,
        scale_mlp,
        shift_mlp,
    )

    normed_two_half = after(normed_two_half, cot_far)
    near, far = gather_eight(normed_two_half, mlp_full)
    mlp_grad, keep, send, activated, fc1_bias_part, fc2_bias_part, _, _ = feed_forward(
        near, far, mlp_full, fc1_bias_here[None], cot_near, cot_far, gate_mlp
    )
    mlp_grad = lax.psum_scatter(mlp_grad, "zz", scatter_dimension=0, tiled=True)
    grad_hidden_half, grad_branch_half, mod_sums = second_backward(
        scatter_eight(keep, send), hidden_half, branch_half, grad_out_half, scale_mlp, gate_attn
    )
    near, far = gather_eight(grad_branch_half)

    grad_in, keep, send, qv_bias_part, grad_branch_all, proj_bias_part = attention_backward(
        near, far, queries, keys, values, attn_full
    )

    out_keep, out_send = feed_forward_out(after(activated, grad_branch_half), mlp_full)
    block_half, gate_sum = second_branch(
        scatter_eight(out_keep, out_send),
        fc2_bias_full[None],
        hidden_half,
        gate_mlp,
        grad_out_half,
    )

    attn_grads = attention_weights(
        after(grad_in, mlp_grad, gate_sum),
        normed_one,
        grad_branch_all,
        attended,
    )
    attn_grad = lax.psum_scatter(attn_grads, "zz", scatter_dimension=0, tiled=True)
    tokens_grad_half, grad_mod = first_backward(
        scatter_eight(keep, after(send, attn_grads)),
        inputs_half,
        grad_hidden_half,
        scale_attn,
        mod_sums,
        gate_sum,
    )

    block_out = true_order(block_half, exchange(block_half, "tensor"))
    tokens_grad = true_order(tokens_grad_half, exchange(tokens_grad_half, "tensor")).astype(f32)
    mlp_parts = send_four(split_four(mlp_grad, place))
    fc1_weight_grad, fc2_weight_grad = unpack(mlp_parts, (1, 1), place)
    grad_mod_other = exchange(after(grad_mod, fc1_weight_grad), "tensor")
    own = 2 * feats + units
    bias_parts = (qv_bias_part, fc1_bias_part, proj_bias_part, fc2_bias_part)
    dealt = deal_columns(grad_mod, grad_mod_other, bias_parts, dp, n_zz)
    own_rows = -(-own // dealt.shape[2])
    dealt = send_zz([dealt[m] for m in range(n_zz)])
    attn_parts = split_four(after(attn_grad, fc1_weight_grad), place)
    dealt, biases = deal_again([after(dealt[0], attn_parts[0])] + dealt[1:], own_rows)
    dealt = jnp.stack(send_four(dealt), axis=1)
    grad_mod_columns = dealt[:n_zz].reshape(n_dp, dealt.shape[2]).astype(bf16)
    mod_bias_grad = jnp.sum(grad_mod_columns.astype(f32), axis=0)
    mod_weight_grad = product(all_silu, grad_mod_columns, "ld,lc->dc")
    grad_silu = product(grad_mod_columns, mod_weight, "lc,dc->ld")
    attn_parts = send_four(attn_parts)
    qkv_weight_grad, proj_weight_grad = unpack(attn_parts, (3, 1), place)
    grad_silu = scatter_dp(grad_silu, proj_weight_grad)
    conditions_grad = jax.vjp(jax.nn.silu, cond_values)[1](grad_silu)[0]

    biases = biases.reshape(-1)
    group_biases = dealt[n_zz:].transpose(1, 0, 2).reshape(GROUP, -1)[:, :own]
    group_biases = reorder(group_biases, place)
    qv_all = jnp.concatenate(
        [group_biases[:, :feats].reshape(-1), group_biases[:, feats : 2 * feats].reshape(-1)]
    )
    fc1_all = group_biases[:, 2 * feats :].reshape(-1)
    proj_all = biases[own : own + width]
    fc2_all = biases[own + width : own + 2 * width]

    def piece(vector):
        size = vector.shape[0] // n_dp
        return lax.dynamic_slice_in_dim(vector, dp * size, size, 0)

    qkv_weight_grad = qkv_weight_grad.transpose(1, 0, 2)
    fc1_weight_grad = fc1_weight_grad[0]
    fc2_weight_grad = fc2_weight_grad[0].T
    proj_weight_grad = proj_weight_grad[0].T
    return (
        block_out,
        tokens_grad,
        conditions_grad,
        mod_weight_grad,
        mod_bias_grad,
        qkv_weight_grad,
        piece(qv_all)[None],
        proj_weight_grad,
        piece(proj_all),
        fc1_weight_grad,
        piece(fc1_all)[None],
        fc2_weight_grad,
        piece(fc2_all),
    )


def solution(mesh):
    n_dp, n_tensor = mesh.shape["dp"], mesh.shape["tensor"]
    cut = Mesh(
        mesh.devices.reshape(n_dp // GROUP, 2, 2, n_tensor), ("zz", "xx", "core", "tensor")
    )
    dp = ("zz", "xx", "core")
    return jax.shard_map(
        local,
        mesh=cut,
        in_specs=(
            P(dp, None),
            P(dp, None),
            P(None, dp),
            P(dp),
            P(dp, None, "tensor"),
            P("tensor", dp),
            P("tensor", dp),
            P(dp),
            P(dp, "tensor"),
            P("tensor", dp),
            P("tensor", dp),
            P(dp),
            P(dp, None),
        ),
        out_specs=(
            P(dp, None),
            P(dp, None),
            P(dp, None),
            P(None, dp),
            P(dp),
            P(dp, None, "tensor"),
            P("tensor", dp),
            P("tensor", dp),
            P(dp),
            P(dp, "tensor"),
            P("tensor", dp),
            P("tensor", dp),
            P(dp),
        ),
        check_vma=False,
    )
```

```python
import jax
import jax.numpy as jnp
from jax import lax
from jax.experimental import pallas as pl
from jax.experimental.pallas import tpu as pltpu
from jax.sharding import Mesh, PartitionSpec as P

HEAD = 72
EPSILON = 1e-06
GROUP = 4
ROOT = 0.7978845608028654
VMEM_LIMIT = 48 * 1024 * 1024

bf16 = jnp.bfloat16
f32 = jnp.float32


def product(left, right, form):
    return jnp.einsum(form, left, right, preferred_element_type=f32)


def exchange(value, axis, mask=1):
    size = lax.axis_size(axis)
    return lax.ppermute(value, axis, [(i, i ^ mask) for i in range(size)])


def reorder(value, position):
    count = value.shape[0]
    bit = 1
    while bit < count:
        parts = value.reshape((count // (2 * bit), 2, bit) + value.shape[1:])
        flip = (position // bit) % 2 == 1
        first = jnp.where(flip, parts[:, 1], parts[:, 0])
        second = jnp.where(flip, parts[:, 0], parts[:, 1])
        value = jnp.stack([first, second], axis=1).reshape(value.shape)
        bit *= 2
    return value


def after(value, *others):
    def nothing(*refs):
        pass

    return pl.pallas_call(
        nothing,
        out_shape=jax.ShapeDtypeStruct(value.shape, value.dtype),
        in_specs=[pl.BlockSpec(memory_space=pl.ANY)] * (1 + len(others)),
        out_specs=pl.BlockSpec(memory_space=pl.ANY),
        input_output_aliases={0: 0},
    )(value, *others)


def send_four(parts):
    return [
        parts[0],
        exchange(parts[1], "core"),
        exchange(parts[2], "xx"),
        exchange(parts[3], ("xx", "core"), 3),
    ]


def send_zz(parts):
    return [parts[0]] + [exchange(parts[m], "zz", m) for m in range(1, len(parts))]


def gather_dp(value):
    four = jnp.concatenate(send_four([value] * GROUP), axis=0)
    return jnp.concatenate(send_zz([four] * lax.axis_size("zz")), axis=0)


def scatter_dp(value, *others):
    steps = lax.axis_size("zz")
    four = sum(send_zz([value[m * GROUP : (m + 1) * GROUP] for m in range(steps)]))
    four = after(four, *others)
    return sum(send_four([four[d : d + 1] for d in range(GROUP)])), four


def gather_four(value):
    near = jnp.concatenate([value, exchange(value, "xx")], axis=0)
    return near, exchange(near, "core")


def gather_eight(value, *others):
    parts = send_plane([value] * 4)

    def kernel(*refs):
        rows = value.shape[0]
        for i in range(4):
            refs[4][i * rows : (i + 1) * rows, :] = refs[i][...]

    near = call(kernel, [((4 * value.shape[0], value.shape[1]), bf16)], parts)[0]
    if others:
        near = after(near, *others)
    return near, exchange(near, "core")


def send_plane(parts):
    return [
        parts[0],
        exchange(parts[1], "tensor"),
        exchange(parts[2], "xx"),
        exchange(parts[3], ("xx", "tensor"), 3),
    ]


def scatter_eight(keep, send):
    rows = keep.shape[0] // 4
    shape = (rows, keep.shape[1])

    def kernel(a, b, own, *sent):
        own[...] = a[:rows, :] + b[:rows, :].astype(f32)
        for i in range(1, 4):
            part = slice(i * rows, (i + 1) * rows)
            sent[i - 1][...] = (a[part, :] + b[part, :].astype(f32)).astype(bf16)

    got = exchange(send, "core")
    return send_plane(call(kernel, [(shape, f32)] + [(shape, bf16)] * 3, (keep, got)))


def total_of(refs):
    own, one, two, three = [ref[...].astype(f32) for ref in refs]
    return (own + one) + (two + three)


def norm(values):
    mean = jnp.mean(values, axis=-1, keepdims=True)
    centered = values - mean
    variance = jnp.mean(centered * centered, axis=-1, keepdims=True)
    inverse = lax.rsqrt(variance + EPSILON)
    return centered * inverse, inverse


def norm_back(grad, normed, inverse, scale):
    scaled = grad * (1.0 + scale)
    mean_scaled = jnp.mean(scaled, axis=-1, keepdims=True)
    mean_product = jnp.mean(scaled * normed, axis=-1, keepdims=True)
    return inverse * (scaled - mean_scaled - normed * mean_product)


def transposed_dot(left, right):
    return lax.dot_general(left, right, (((0,), (0,)), ((), ())), preferred_element_type=f32)


def dot_rows(left, right):
    return lax.dot_general(left, right, (((1,), (1,)), ((), ())), preferred_element_type=f32)


def dot(left, right):
    return lax.dot_general(left, right, (((1,), (0,)), ((), ())), preferred_element_type=f32)


def call(kernel, outs, args, flops=0):
    return pl.pallas_call(
        kernel,
        out_shape=[jax.ShapeDtypeStruct(shape, dtype) for shape, dtype in outs],
        in_specs=[pl.BlockSpec(memory_space=pltpu.VMEM)] * len(args),
        out_specs=[pl.BlockSpec(memory_space=pltpu.VMEM)] * len(outs),
        compiler_params=pltpu.CompilerParams(vmem_limit_bytes=VMEM_LIMIT),
        cost_estimate=pl.CostEstimate(flops=flops, bytes_accessed=0, transcendentals=0),
    )(*args)


def place_call(kernel, outs, args, place, *scratch):
    return pl.pallas_call(
        kernel,
        out_shape=[jax.ShapeDtypeStruct(shape, dtype) for shape, dtype in outs],
        in_specs=[pl.BlockSpec(memory_space=pltpu.SMEM)]
        + [pl.BlockSpec(memory_space=pltpu.VMEM)] * len(args),
        out_specs=[pl.BlockSpec(memory_space=pltpu.VMEM)] * len(outs),
        scratch_shapes=scratch,
        compiler_params=pltpu.CompilerParams(vmem_limit_bytes=VMEM_LIMIT),
        cost_estimate=pl.CostEstimate(flops=0, bytes_accessed=0, transcendentals=0),
    )(place.reshape(1), *args)


def pack(arrays, place):
    rows, width = arrays[0].shape[-2], arrays[0].shape[-1] // GROUP
    counts = [1 if value.ndim == 2 else value.shape[0] for value in arrays]
    total = sum(counts)

    def kernel(at, *refs):
        chunks = refs[-1]
        i = 0
        for ref, count in zip(refs, counts):
            for j in range(count):
                for s in range(GROUP):
                    columns = slice(s * width, (s + 1) * width)
                    value = ref[:, columns] if len(ref.shape) == 2 else ref[j, :, columns]
                    chunks[s, :, i * width : (i + 1) * width] = value
                i += 1
        for d in range(GROUP):
            refs[len(arrays) + d][...] = chunks[at[0] ^ d]

    shape = (rows, total * width)
    return place_call(
        kernel,
        [(shape, bf16)] * GROUP,
        arrays,
        place,
        pltpu.VMEM((GROUP,) + shape, bf16),
    )


def join(parts, place):
    def kernel(at, *refs):
        for d in range(GROUP):
            refs[GROUP][at[0] ^ d] = refs[d][...]

    rows, width = parts[0].shape
    joined = place_call(kernel, [((GROUP, rows, width), bf16)], parts, place)[0]
    return joined.reshape(GROUP * rows, width)


def unpack(parts, counts, place):
    rows, width = parts[0].shape
    width = width // sum(counts)

    def kernel(at, *refs):
        chunks = refs[-1]
        for d in range(GROUP):
            chunks[at[0] ^ d] = refs[d][...].astype(f32)
        i = 0
        for ref, count in zip(refs[GROUP:], counts):
            for j in range(count):
                for s in range(GROUP):
                    columns = slice(s * width, (s + 1) * width)
                    ref[j, :, columns] = chunks[s, :, i * width : (i + 1) * width]
                i += 1

    return place_call(
        kernel,
        [((count, rows, GROUP * width), f32) for count in counts],
        parts,
        place,
        pltpu.VMEM((GROUP, rows, sum(counts) * width), f32),
    )


def collect_rows(pieces, dp, width):
    steps, _, columns = pieces[0].shape

    def kernel(at, *refs):
        blocks, flat = refs[-2], refs[-1]
        for d in range(GROUP):
            for m in range(steps):
                rows = [refs[d][m, i ^ d : (i ^ d) + 1, :] for i in (0, 2, 1, 3)]
                blocks[at[0] ^ (m * GROUP + d)] = jnp.concatenate(rows, axis=0)
        for k in range(steps * GROUP):
            flat[:, k * columns : (k + 1) * columns] = blocks[k]
        for i in range(6):
            refs[GROUP + i][...] = flat[:, i * width : (i + 1) * width]

    return place_call(
        kernel,
        [((GROUP, width), f32)] * 6,
        pieces,
        dp,
        pltpu.VMEM((steps * GROUP, GROUP, columns), f32),
        pltpu.VMEM((GROUP, 6 * width), f32),
    )


def deal_columns(own, other, biases, dp, steps):
    width = own.shape[1]
    columns = 6 * width // (steps * GROUP)
    extra = -(-sum(value.size for value in biases) // columns)

    def kernel(at, a, b, *refs):
        out, blocks, flat, flat_bias = refs[-4:]
        for i in range(6):
            flat[:, i * width : (i + 1) * width] = a[i : i + 1, :] + b[i : i + 1, :]
        for k in range(steps * GROUP):
            blocks[k] = flat[:, k * columns : (k + 1) * columns]
        flat_bias[...] = jnp.zeros_like(flat_bias)
        start = 0
        for ref in refs[: len(biases)]:
            for i in range(ref.shape[0]):
                flat_bias[:, start : start + ref.shape[1]] = ref[i : i + 1, :]
                start += ref.shape[1]
        for m in range(steps):
            for d in range(GROUP):
                out[m, d : d + 1, :] = blocks[at[0] ^ (m * GROUP + d)]
            for r in range(extra):
                part = flat_bias[:, r * columns : (r + 1) * columns]
                out[m, GROUP + r : GROUP + r + 1, :] = part

    return place_call(
        kernel,
        [((steps, GROUP + extra, columns), f32)],
        (own, other, *biases),
        dp,
        pltpu.VMEM((steps * GROUP, 1, columns), f32),
        pltpu.VMEM((1, 6 * width), f32),
        pltpu.VMEM((1, extra * columns), f32),
    )[0]


def deal_again(pieces, count):
    steps = len(pieces)
    columns = pieces[0].shape[1]
    extra = pieces[0].shape[0] - GROUP

    def kernel(*refs):
        sums = refs[0][GROUP:, :]
        for m in range(1, steps):
            sums = sums + refs[m][GROUP:, :]
        refs[-1][...] = sums
        for d in range(GROUP):
            out = refs[steps + d]
            for m in range(steps):
                out[m : m + 1, :] = refs[m][d : d + 1, :]
            out[steps:, :] = sums[:count, :]

    outs = call(
        kernel,
        [((steps + count, columns), f32)] * GROUP + [((extra, columns), f32)],
        pieces,
    )
    return outs[:GROUP], outs[GROUP]


def split_four(value, place):
    rows = value.shape[0] // GROUP
    chunks = value.reshape(GROUP, rows, value.shape[1])

    def kernel(at, *refs):
        for d in range(GROUP):
            refs[1 + d][...] = refs[0][at[0] ^ d]

    return place_call(kernel, [((rows, value.shape[1]), bf16)] * GROUP, [chunks], place)


def row_sum(value):
    return jnp.sum(value, axis=0, keepdims=True)


def first_branch(parts, bias, inputs, gate, scale, shift):
    shape = inputs.shape

    def kernel(a, b, c, d, bi, x, g, sc, sh, branch_out, hidden_out, normed_out):
        branch = total_of((a, b, c, d)) + bi[...]
        hidden = x[...].astype(f32) + g[0:1, :] * branch
        branch_out[...] = branch
        hidden_out[...] = hidden
        normed_out[...] = (norm(hidden)[0] * (1.0 + sc[0:1, :]) + sh[0:1, :]).astype(bf16)

    return call(
        kernel,
        [(shape, f32), (shape, f32), (shape, bf16)],
        (*parts, bias, inputs, gate, scale, shift),
    )


def second_backward(parts, hidden, branch, cot, scale, gate):
    shape = hidden.shape

    def kernel(a, b, c, d, h, br, g, sc, gt, hidden_out, branch_out, sums):
        grad = total_of((a, b, c, d))
        normed, inverse = norm(h[...])
        grad_hidden = g[...].astype(f32) + norm_back(grad, normed, inverse, sc[0:1, :])
        hidden_out[...] = grad_hidden
        branch_out[...] = (gt[0:1, :] * grad_hidden).astype(bf16)
        sums[0:1, :] = row_sum(grad_hidden * br[...])
        sums[1:2, :] = row_sum(grad)
        sums[2:3, :] = row_sum(grad * normed)

    return call(
        kernel,
        [(shape, f32), (shape, bf16), ((3, shape[1]), f32)],
        (*parts, hidden, branch, cot, scale, gate),
    )


def second_branch(parts, bias, hidden, gate, cot):
    shape = hidden.shape

    def kernel(a, b, c, d, bi, h, gt, g, out, gate_sum):
        branch = total_of((a, b, c, d)) + bi[...]
        out[...] = (h[...] + gt[0:1, :] * branch).astype(bf16)
        gate_sum[...] = row_sum(g[...].astype(f32) * branch)

    return call(
        kernel, [(shape, bf16), ((1, shape[1]), f32)], (*parts, bias, hidden, gate, cot)
    )


def first_backward(parts, inputs, grad_hidden, scale, sums, gate_sum):
    shape = inputs.shape

    def kernel(a, b, c, d, x, gh, sc, s, gs, out, mod):
        grad = total_of((a, b, c, d))
        normed, inverse = norm(x[...].astype(f32))
        out[...] = (gh[...] + norm_back(grad, normed, inverse, sc[0:1, :])).astype(bf16)
        mod[0:1, :] = row_sum(grad)
        mod[1:2, :] = row_sum(grad * normed)
        mod[2:5, :] = s[...]
        mod[5:6, :] = gs[...]

    return call(
        kernel,
        [(shape, bf16), ((6, shape[1]), f32)],
        (*parts, inputs, grad_hidden, scale, sums, gate_sum),
    )


def head_masks(feats):
    lane = lax.broadcasted_iota(jnp.int32, (1, feats), 1)
    return [(lane >= h * HEAD) & (lane < (h + 1) * HEAD) for h in range(feats // HEAD)]


def only(mask, value):
    return jnp.where(mask, value, jnp.zeros_like(value))


def split_store(keep_ref, send_ref, value):
    half = value.shape[0] // 2
    keep_ref[...] = value[:half]
    send_ref[...] = value[half:].astype(bf16)


def attention_forward(near, far, shift, scale, weights, biases):
    total, width = 2 * near.shape[0], near.shape[1]
    feats = biases.shape[1]
    seq = total // GROUP
    factor = HEAD ** (-0.5)

    def kernel(t_near, t_far, sh, sc, w, b, normed, q_out, k_out, v_out, att, keep, send):
        for i in range(GROUP):
            rows = slice(i * seq, (i + 1) * seq)
            tok = t_near if i < GROUP // 2 else t_far
            value = norm(tok[i % 2 * seq : (i % 2 + 1) * seq, :].astype(f32))[0]
            normed[rows, :] = (value * (1.0 + sc[i : i + 1, :]) + sh[i : i + 1, :]).astype(bf16)
        projected = dot(normed[...], w[:, : 3 * feats])
        q_out[...] = (projected[:, :feats] + b[0:1, :]).astype(bf16)
        k_out[...] = projected[:, feats : 2 * feats].astype(bf16)
        v_out[...] = (projected[:, 2 * feats :] + b[1:2, :]).astype(bf16)
        masks = head_masks(feats)
        for i in range(GROUP):
            rows = slice(i * seq, (i + 1) * seq)
            q, k, v = q_out[rows, :], k_out[rows, :], v_out[rows, :]
            result = jnp.zeros((seq, feats), f32)
            for mask in masks:
                probs = softmax(dot_rows(only(mask, q), k) * factor)
                result += dot(probs.astype(bf16), only(mask, v))
            att[rows, :] = result.astype(bf16)
        split_store(keep, send, dot_rows(att[...], w[:, 3 * feats :]))

    return call(
        kernel,
        [
            ((total, width), bf16),
            ((total, feats), bf16),
            ((total, feats), bf16),
            ((total, feats), bf16),
            ((total, feats), bf16),
            ((total // 2, width), f32),
            ((total // 2, width), bf16),
        ],
        (near, far, shift, scale, weights, biases),
    )


def softmax(scores):
    exponent = jnp.exp(scores - jnp.max(scores, axis=-1, keepdims=True))
    return exponent / jnp.sum(exponent, axis=-1, keepdims=True)


def symmetric_sum(parts):
    pairs = [parts[2 * i] + parts[2 * i + 1] for i in range(GROUP)]
    return (pairs[0] + pairs[1]) + (pairs[2] + pairs[3])


def attention_backward(near, far, q_all, k_all, v_all, weights):
    total = q_all.shape[0]
    width, feats = weights.shape[0], q_all.shape[1]
    seq = total // GROUP
    factor = HEAD ** (-0.5)

    def kernel(g_near, g_far, q_in, k_in, v_in, w, grad_in, keep, send, bias, g, proj_bias):
        masks = head_masks(feats)
        g[: total // 2, :] = g_near[...]
        g[total // 2 :, :] = g_far[...]
        half = seq // 2
        proj_bias[...] = symmetric_sum(
            [row_sum(g[i * half : (i + 1) * half, :].astype(f32)) for i in range(2 * GROUP)]
        )
        grad_att = dot(g[...], w[:, 3 * feats :]).astype(bf16)
        q_sum = jnp.zeros((1, feats), f32)
        v_sum = jnp.zeros((1, feats), f32)
        for i in range(GROUP):
            rows = slice(i * seq, (i + 1) * seq)
            q, k, v = q_in[rows, :], k_in[rows, :], v_in[rows, :]
            ga = grad_att[rows, :]
            gq = jnp.zeros((seq, feats), f32)
            gk = jnp.zeros((seq, feats), f32)
            gv = jnp.zeros((seq, feats), f32)
            for mask in masks:
                probs = softmax(dot_rows(only(mask, q), k) * factor)
                gv += only(mask, transposed_dot(probs.astype(bf16), ga))
                gp = dot_rows(only(mask, ga), v)
                gs = probs * (gp - jnp.sum(probs * gp, axis=-1, keepdims=True))
                gs = gs.astype(bf16)
                gq += only(mask, dot(gs, k))
                gk += only(mask, transposed_dot(gs, q))
            gq, gk = gq * factor, gk * factor
            q_sum += jnp.sum(gq, axis=0, keepdims=True)
            v_sum += jnp.sum(gv, axis=0, keepdims=True)
            grad_in[rows, :] = jnp.concatenate([gq, gk, gv], axis=1).astype(bf16)
        bias[0:1, :] = q_sum
        bias[1:2, :] = v_sum
        split_store(keep, send, dot_rows(grad_in[...], w[:, : 3 * feats]))

    return call(
        kernel,
        [
            ((total, 3 * feats), bf16),
            ((total // 2, width), f32),
            ((total // 2, width), bf16),
            ((2, feats), f32),
            ((total, width), bf16),
            ((1, width), f32),
        ],
        (near, far, q_all, k_all, v_all, weights),
    )


def attention_weights(grad_in, normed, grad_branch, att):
    width, feats = normed.shape[1], att.shape[1]

    def kernel(gi, n, g, a, grads):
        grads[:, : 3 * feats] = transposed_dot(n[...], gi[...]).astype(bf16)
        grads[:, 3 * feats :] = transposed_dot(g[...], a[...]).astype(bf16)

    return call(kernel, [((width, 4 * feats), bf16)], (grad_in, normed, grad_branch, att))[0]


def feed_forward(near, far, weights, bias, cot_near, cot_far, gate):
    total, width = 2 * near.shape[0], near.shape[1]
    units = weights.shape[1] // 2
    seq = total // GROUP

    def kernel(
        n_near, n_far, w, b, c_near, c_far, gt, grads, keep, send, act_out, bias_out, fc2_out, grad_out, n
    ):
        n[: total // 2, :] = n_near[...]
        n[total // 2 :, :] = n_far[...]
        sums = []
        half = seq // 2
        for i in range(2 * GROUP):
            c = c_near if i < GROUP else c_far
            value = c[i % GROUP * half : (i % GROUP + 1) * half, :].astype(f32)
            value = value * gt[i // 2 : i // 2 + 1, :]
            sums.append(row_sum(value))
            grad_out[i * half : (i + 1) * half, :] = value.astype(bf16)
        fc2_out[...] = symmetric_sum(sums)
        pre = dot(n[...], w[:, :units]) + b[...]
        inner = ROOT * (pre + 0.044715 * (pre * pre * pre))
        tanh = jnp.tanh(inner)
        act = (0.5 * pre * (1.0 + tanh)).astype(bf16)
        slope = 0.5 * (1.0 + tanh) + 0.5 * pre * (1.0 - tanh * tanh) * (
            ROOT * (1.0 + 3 * 0.044715 * (pre * pre))
        )
        grad_pre = dot(grad_out[...], w[:, units:]) * slope
        bias_out[...] = jnp.sum(grad_pre, axis=0, keepdims=True)
        grad_pre = grad_pre.astype(bf16)
        grads[:, units:] = transposed_dot(grad_out[...], act).astype(bf16)
        grads[:, :units] = transposed_dot(n[...], grad_pre).astype(bf16)
        split_store(keep, send, dot_rows(grad_pre, w[:, :units]))
        act_out[...] = act

    return call(
        kernel,
        [
            ((width, 2 * units), bf16),
            ((total // 2, width), f32),
            ((total // 2, width), bf16),
            ((total, units), bf16),
            ((1, units), f32),
            ((1, width), f32),
            ((total, width), bf16),
            ((total, width), bf16),
        ],
        (near, far, weights, bias, cot_near, cot_far, gate),
    )


def feed_forward_out(act, weights):
    total, units = act.shape
    width = weights.shape[0]

    def kernel(a, w, keep, send):
        split_store(keep, send, dot_rows(a[...], w[:, units:]))

    return call(
        kernel,
        [((total // 2, width), f32), ((total // 2, width), bf16)],
        (act, weights),
    )


def local(
    tokens,
    conditions,
    mod_weight,
    mod_bias,
    qkv_weight,
    qv_bias,
    proj_weight,
    proj_bias,
    fc1_weight,
    fc1_bias,
    fc2_weight,
    fc2_bias,
    cotangent,
):
    seq, width = tokens.shape
    rows = seq // 2
    d_rows = qkv_weight.shape[0]
    t_width = qkv_weight.shape[2]
    hidden = fc1_weight.shape[1]
    feats = t_width // GROUP
    units = hidden // GROUP
    n_dp = width // d_rows
    t = lax.axis_index("tensor")
    place = lax.axis_index("xx") * 2 + lax.axis_index("core")
    dp = lax.axis_index("zz") * GROUP + place

    attn_arrays = [qkv_weight.transpose(1, 0, 2), proj_weight.T]
    attn_part = join(send_four(pack(attn_arrays, place)), place)
    attn_full = lax.all_gather(attn_part, "zz", axis=0, tiled=True)

    cond_values = conditions.astype(f32)
    silu_conds = jax.nn.silu(cond_values).astype(bf16)
    small = jnp.concatenate(
        [silu_conds, qv_bias, proj_bias[None], fc1_bias, fc2_bias[None]], axis=1
    )
    small = gather_dp(after(small, attn_part))
    all_silu = small[:, :width]
    spots = jnp.arange(n_dp)
    order = ((spots[:, None] ^ dp) == spots[None]).astype(bf16)
    biases = product(order, small[:, width:], "ij,jc->ic")
    n_qv, n_b, n_f = qv_bias.shape[1], proj_bias.shape[0], fc1_bias.shape[1]
    cuts = [n_qv, n_qv + n_b, n_qv + n_b + n_f]
    qv_full = biases[:, : cuts[0]].reshape(2, GROUP, feats)
    proj_bias_full = biases[:, cuts[0] : cuts[1]].reshape(width)
    fc1_bias_full = biases[:, cuts[1] : cuts[2]].reshape(GROUP, units)
    fc2_bias_full = biases[:, cuts[2] :].reshape(width)
    qv_here = lax.dynamic_index_in_dim(qv_full, place, 1, keepdims=False)
    fc1_bias_here = lax.dynamic_index_in_dim(fc1_bias_full, place, 0, keepdims=False)
    mod_columns = product(all_silu, mod_weight, "ld,dc->lc") + mod_bias.astype(f32)
    n_zz = n_dp // GROUP
    mod_parts = send_zz([mod_columns[m * GROUP : (m + 1) * GROUP] for m in range(n_zz)])
    mod_parts = after(jnp.stack(mod_parts), attn_full)
    mod_parts = send_four([mod_parts] * GROUP)
    modulation = collect_rows(mod_parts, dp, width)
    shift_attn, scale_attn, gate_attn, shift_mlp, scale_mlp, gate_mlp = modulation
    mlp_arrays = [fc1_weight, fc2_weight.T]
    mlp_part = join(send_four(pack(mlp_arrays, place)), place)
    mlp_full = lax.all_gather(mlp_part, "zz", axis=0, tiled=True)
    def own_order(value):
        first = lax.dynamic_slice_in_dim(value, t * rows, rows, 0)
        second = lax.dynamic_slice_in_dim(value, (1 - t) * rows, rows, 0)
        return jnp.concatenate([first, second], axis=0)

    def true_order(own, other):
        return jnp.where(
            t == 0,
            jnp.concatenate([own, other], axis=0),
            jnp.concatenate([other, own], axis=0),
        )

    tokens_own = own_order(tokens)
    cot_own = after(own_order(cotangent), mod_columns)
    tokens_near, tokens_far = gather_four(tokens_own)
    cot_near, cot_far = gather_four(cot_own)
    inputs_half = tokens_own[:rows]
    grad_out_half = cot_own[:rows]

    normed_one, queries, keys, values, attended, keep, send = attention_forward(
        tokens_near, tokens_far, shift_attn, scale_attn, attn_full, qv_here
    )
    branch_half, hidden_half, normed_two_half = first_branch(
        scatter_eight(keep, send),
        proj_bias_full[None],
        inputs_half,
        gate_attn,
        scale_mlp,
        shift_mlp,
    )

    normed_two_half = after(normed_two_half, cot_far)
    near, far = gather_eight(normed_two_half)
    mlp_grad, keep, send, activated, fc1_bias_part, fc2_bias_part, _, _ = feed_forward(
        near, far, mlp_full, fc1_bias_here[None], cot_near, cot_far, gate_mlp
    )
    mlp_grad = lax.psum_scatter(mlp_grad, "zz", scatter_dimension=0, tiled=True)
    grad_hidden_half, grad_branch_half, mod_sums = second_backward(
        scatter_eight(keep, send), hidden_half, branch_half, grad_out_half, scale_mlp, gate_attn
    )
    near, far = gather_eight(grad_branch_half)

    grad_in, keep, send, qv_bias_part, grad_branch_all, proj_bias_part = attention_backward(
        near, far, queries, keys, values, attn_full
    )

    out_keep, out_send = feed_forward_out(after(activated, grad_branch_half), mlp_full)
    block_half, gate_sum = second_branch(
        scatter_eight(out_keep, out_send),
        fc2_bias_full[None],
        hidden_half,
        gate_mlp,
        grad_out_half,
    )

    attn_grads = attention_weights(
        after(grad_in, gate_sum), normed_one, grad_branch_all, attended
    )
    attn_grads = after(attn_grads, mlp_grad)
    attn_grad = lax.psum_scatter(attn_grads, "zz", scatter_dimension=0, tiled=True)
    tokens_grad_half, grad_mod = first_backward(
        scatter_eight(keep, after(send, attn_grads)),
        inputs_half,
        grad_hidden_half,
        scale_attn,
        mod_sums,
        gate_sum,
    )

    block_out = true_order(block_half, exchange(block_half, "tensor"))
    tokens_grad = true_order(tokens_grad_half, exchange(tokens_grad_half, "tensor")).astype(f32)
    mlp_parts = send_four(split_four(mlp_grad, place))
    fc1_weight_grad, fc2_weight_grad = unpack(mlp_parts, (1, 1), place)
    grad_mod_other = exchange(after(grad_mod, fc1_weight_grad), "tensor")
    own = 2 * feats + units
    bias_parts = (qv_bias_part, fc1_bias_part, proj_bias_part, fc2_bias_part)
    dealt = deal_columns(grad_mod, grad_mod_other, bias_parts, dp, n_zz)
    own_rows = -(-own // dealt.shape[2])
    dealt = send_zz([dealt[m] for m in range(n_zz)])
    attn_parts = split_four(after(attn_grad, fc1_weight_grad), place)
    dealt, biases = deal_again(dealt, own_rows)
    dealt = send_four(dealt)
    dealt = jnp.stack([after(dealt[0], attn_parts[0])] + dealt[1:], axis=1)
    grad_mod_columns = dealt[:n_zz].reshape(n_dp, dealt.shape[2]).astype(bf16)
    mod_bias_grad = jnp.sum(grad_mod_columns.astype(f32), axis=0)
    grad_silu = product(grad_mod_columns, mod_weight, "lc,dc->ld")
    attn_parts = send_four(attn_parts)
    qkv_weight_grad, proj_weight_grad = unpack(attn_parts, (3, 1), place)
    grad_silu, near_sum = scatter_dp(grad_silu, proj_weight_grad)
    mod_weight_grad = product(all_silu, after(grad_mod_columns, near_sum), "ld,lc->dc")
    conditions_grad = jax.vjp(jax.nn.silu, cond_values)[1](grad_silu)[0]

    biases = biases.reshape(-1)
    group_biases = dealt[n_zz:].transpose(1, 0, 2).reshape(GROUP, -1)[:, :own]
    group_biases = reorder(group_biases, place)
    qv_all = jnp.concatenate(
        [group_biases[:, :feats].reshape(-1), group_biases[:, feats : 2 * feats].reshape(-1)]
    )
    fc1_all = group_biases[:, 2 * feats :].reshape(-1)
    proj_all = biases[own : own + width]
    fc2_all = biases[own + width : own + 2 * width]

    def piece(vector):
        size = vector.shape[0] // n_dp
        return lax.dynamic_slice_in_dim(vector, dp * size, size, 0)

    qkv_weight_grad = qkv_weight_grad.transpose(1, 0, 2)
    fc1_weight_grad = fc1_weight_grad[0]
    fc2_weight_grad = fc2_weight_grad[0].T
    proj_weight_grad = proj_weight_grad[0].T
    return (
        block_out,
        tokens_grad,
        conditions_grad,
        mod_weight_grad,
        mod_bias_grad,
        qkv_weight_grad,
        piece(qv_all)[None],
        proj_weight_grad,
        piece(proj_all),
        fc1_weight_grad,
        piece(fc1_all)[None],
        fc2_weight_grad,
        piece(fc2_all),
    )


def solution(mesh):
    n_dp, n_tensor = mesh.shape["dp"], mesh.shape["tensor"]
    cut = Mesh(
        mesh.devices.reshape(n_dp // GROUP, 2, 2, n_tensor), ("zz", "xx", "core", "tensor")
    )
    dp = ("zz", "xx", "core")
    return jax.shard_map(
        local,
        mesh=cut,
        in_specs=(
            P(dp, None),
            P(dp, None),
            P(None, dp),
            P(dp),
            P(dp, None, "tensor"),
            P("tensor", dp),
            P("tensor", dp),
            P(dp),
            P(dp, "tensor"),
            P("tensor", dp),
            P("tensor", dp),
            P(dp),
            P(dp, None),
        ),
        out_specs=(
            P(dp, None),
            P(dp, None),
            P(dp, None),
            P(None, dp),
            P(dp),
            P(dp, None, "tensor"),
            P("tensor", dp),
            P("tensor", dp),
            P(dp),
            P(dp, "tensor"),
            P("tensor", dp),
            P("tensor", dp),
            P(dp),
        ),
        check_vma=False,
    )
```

```python
import jax
import jax.numpy as jnp
from jax import lax
from jax.experimental import pallas as pl
from jax.experimental.pallas import tpu as pltpu
from jax.sharding import Mesh, PartitionSpec as P

HEAD = 72
EPSILON = 1e-06
GROUP = 4
ROOT = 0.7978845608028654
VMEM_LIMIT = 48 * 1024 * 1024

bf16 = jnp.bfloat16
f32 = jnp.float32


def product(left, right, form):
    return jnp.einsum(form, left, right, preferred_element_type=f32)


def exchange(value, axis, mask=1):
    size = lax.axis_size(axis)
    return lax.ppermute(value, axis, [(i, i ^ mask) for i in range(size)])


def reorder(value, position):
    count = value.shape[0]
    bit = 1
    while bit < count:
        parts = value.reshape((count // (2 * bit), 2, bit) + value.shape[1:])
        flip = (position // bit) % 2 == 1
        first = jnp.where(flip, parts[:, 1], parts[:, 0])
        second = jnp.where(flip, parts[:, 0], parts[:, 1])
        value = jnp.stack([first, second], axis=1).reshape(value.shape)
        bit *= 2
    return value


def after(value, *others):
    def nothing(*refs):
        pass

    return pl.pallas_call(
        nothing,
        out_shape=jax.ShapeDtypeStruct(value.shape, value.dtype),
        in_specs=[pl.BlockSpec(memory_space=pl.ANY)] * (1 + len(others)),
        out_specs=pl.BlockSpec(memory_space=pl.ANY),
        input_output_aliases={0: 0},
    )(value, *others)


def send_four(parts):
    return [
        parts[0],
        exchange(parts[1], "core"),
        exchange(parts[2], "xx"),
        exchange(parts[3], ("xx", "core"), 3),
    ]


def send_zz(parts):
    return [parts[0]] + [exchange(parts[m], "zz", m) for m in range(1, len(parts))]


def gather_dp(value):
    four = jnp.concatenate(send_four([value] * GROUP), axis=0)
    return jnp.concatenate(send_zz([four] * lax.axis_size("zz")), axis=0)


def scatter_dp(value, *others):
    steps = lax.axis_size("zz")
    four = sum(send_zz([value[m * GROUP : (m + 1) * GROUP] for m in range(steps)]))
    four = after(four, *others)
    return sum(send_four([four[d : d + 1] for d in range(GROUP)])), four


def gather_four(value):
    near = jnp.concatenate([value, exchange(value, "xx")], axis=0)
    return near, exchange(near, "core")


def gather_eight(value, *others):
    parts = send_plane([value] * 4)

    def kernel(*refs):
        rows = value.shape[0]
        for i in range(4):
            refs[4][i * rows : (i + 1) * rows, :] = refs[i][...]

    near = call(kernel, [((4 * value.shape[0], value.shape[1]), bf16)], parts)[0]
    if others:
        near = after(near, *others)
    return near, exchange(near, "core")


def send_plane(parts):
    return [
        parts[0],
        exchange(parts[1], "tensor"),
        exchange(parts[2], "xx"),
        exchange(parts[3], ("xx", "tensor"), 3),
    ]


def scatter_eight(keep, send):
    rows = keep.shape[0] // 4
    shape = (rows, keep.shape[1])

    def kernel(a, b, own, *sent):
        own[...] = a[:rows, :] + b[:rows, :].astype(f32)
        for i in range(1, 4):
            part = slice(i * rows, (i + 1) * rows)
            sent[i - 1][...] = (a[part, :] + b[part, :].astype(f32)).astype(bf16)

    got = exchange(send, "core")
    return send_plane(call(kernel, [(shape, f32)] + [(shape, bf16)] * 3, (keep, got)))


def total_of(refs):
    own, one, two, three = [ref[...].astype(f32) for ref in refs]
    return (own + one) + (two + three)


def norm(values):
    mean = jnp.mean(values, axis=-1, keepdims=True)
    centered = values - mean
    variance = jnp.mean(centered * centered, axis=-1, keepdims=True)
    inverse = lax.rsqrt(variance + EPSILON)
    return centered * inverse, inverse


def norm_back(grad, normed, inverse, scale):
    scaled = grad * (1.0 + scale)
    mean_scaled = jnp.mean(scaled, axis=-1, keepdims=True)
    mean_product = jnp.mean(scaled * normed, axis=-1, keepdims=True)
    return inverse * (scaled - mean_scaled - normed * mean_product)


def transposed_dot(left, right):
    return lax.dot_general(left, right, (((0,), (0,)), ((), ())), preferred_element_type=f32)


def dot_rows(left, right):
    return lax.dot_general(left, right, (((1,), (1,)), ((), ())), preferred_element_type=f32)


def dot(left, right):
    return lax.dot_general(left, right, (((1,), (0,)), ((), ())), preferred_element_type=f32)


def call(kernel, outs, args, *scratch):
    return pl.pallas_call(
        kernel,
        out_shape=[jax.ShapeDtypeStruct(shape, dtype) for shape, dtype in outs],
        in_specs=[pl.BlockSpec(memory_space=pltpu.VMEM)] * len(args),
        out_specs=[pl.BlockSpec(memory_space=pltpu.VMEM)] * len(outs),
        scratch_shapes=scratch,
        compiler_params=pltpu.CompilerParams(vmem_limit_bytes=VMEM_LIMIT),
        cost_estimate=pl.CostEstimate(flops=0, bytes_accessed=0, transcendentals=0),
    )(*args)


def place_call(kernel, outs, args, place, *scratch):
    return pl.pallas_call(
        kernel,
        out_shape=[jax.ShapeDtypeStruct(shape, dtype) for shape, dtype in outs],
        in_specs=[pl.BlockSpec(memory_space=pltpu.SMEM)]
        + [pl.BlockSpec(memory_space=pltpu.VMEM)] * len(args),
        out_specs=[pl.BlockSpec(memory_space=pltpu.VMEM)] * len(outs),
        scratch_shapes=scratch,
        compiler_params=pltpu.CompilerParams(vmem_limit_bytes=VMEM_LIMIT),
        cost_estimate=pl.CostEstimate(flops=0, bytes_accessed=0, transcendentals=0),
    )(place.reshape(1), *args)


def pack(arrays, place):
    rows, width = arrays[0].shape[-2], arrays[0].shape[-1] // GROUP
    counts = [1 if value.ndim == 2 else value.shape[0] for value in arrays]
    total = sum(counts)

    def kernel(at, *refs):
        chunks = refs[-1]
        i = 0
        for ref, count in zip(refs, counts):
            for j in range(count):
                for s in range(GROUP):
                    columns = slice(s * width, (s + 1) * width)
                    value = ref[:, columns] if len(ref.shape) == 2 else ref[j, :, columns]
                    chunks[s, :, i * width : (i + 1) * width] = value
                i += 1
        for d in range(GROUP):
            refs[len(arrays) + d][...] = chunks[at[0] ^ d]

    shape = (rows, total * width)
    return place_call(
        kernel,
        [(shape, bf16)] * GROUP,
        arrays,
        place,
        pltpu.VMEM((GROUP,) + shape, bf16),
    )


def join(parts, place):
    def kernel(at, *refs):
        for d in range(GROUP):
            refs[GROUP][at[0] ^ d] = refs[d][...]

    rows, width = parts[0].shape
    joined = place_call(kernel, [((GROUP, rows, width), bf16)], parts, place)[0]
    return joined.reshape(GROUP * rows, width)


def unpack(parts, counts, place):
    rows, width = parts[0].shape
    width = width // sum(counts)

    def kernel(at, *refs):
        chunks = refs[-1]
        for d in range(GROUP):
            chunks[at[0] ^ d] = refs[d][...].astype(f32)
        i = 0
        for ref, count in zip(refs[GROUP:], counts):
            for j in range(count):
                for s in range(GROUP):
                    columns = slice(s * width, (s + 1) * width)
                    ref[j, :, columns] = chunks[s, :, i * width : (i + 1) * width]
                i += 1

    return place_call(
        kernel,
        [((count, rows, GROUP * width), f32) for count in counts],
        parts,
        place,
        pltpu.VMEM((GROUP, rows, sum(counts) * width), f32),
    )


def collect_rows(pieces, dp, width):
    steps, _, columns = pieces[0].shape

    def kernel(at, *refs):
        blocks, flat = refs[-2], refs[-1]
        for d in range(GROUP):
            for m in range(steps):
                rows = [refs[d][m, i ^ d : (i ^ d) + 1, :] for i in (0, 2, 1, 3)]
                blocks[at[0] ^ (m * GROUP + d)] = jnp.concatenate(rows, axis=0)
        for k in range(steps * GROUP):
            flat[:, k * columns : (k + 1) * columns] = blocks[k]
        for i in range(6):
            refs[GROUP + i][...] = flat[:, i * width : (i + 1) * width]

    return place_call(
        kernel,
        [((GROUP, width), f32)] * 6,
        pieces,
        dp,
        pltpu.VMEM((steps * GROUP, GROUP, columns), f32),
        pltpu.VMEM((GROUP, 6 * width), f32),
    )


def deal_columns(own, other, biases, dp, steps):
    width = own.shape[1]
    columns = 6 * width // (steps * GROUP)
    extra = -(-sum(value.size for value in biases) // columns)

    def kernel(at, a, b, *refs):
        out, blocks, flat, flat_bias = refs[-4:]
        for i in range(6):
            flat[:, i * width : (i + 1) * width] = a[i : i + 1, :] + b[i : i + 1, :]
        for k in range(steps * GROUP):
            blocks[k] = flat[:, k * columns : (k + 1) * columns]
        flat_bias[...] = jnp.zeros_like(flat_bias)
        start = 0
        for ref in refs[: len(biases)]:
            for i in range(ref.shape[0]):
                flat_bias[:, start : start + ref.shape[1]] = ref[i : i + 1, :]
                start += ref.shape[1]
        for m in range(steps):
            for d in range(GROUP):
                out[m, d : d + 1, :] = blocks[at[0] ^ (m * GROUP + d)]
            for r in range(extra):
                part = flat_bias[:, r * columns : (r + 1) * columns]
                out[m, GROUP + r : GROUP + r + 1, :] = part

    return place_call(
        kernel,
        [((steps, GROUP + extra, columns), f32)],
        (own, other, *biases),
        dp,
        pltpu.VMEM((steps * GROUP, 1, columns), f32),
        pltpu.VMEM((1, 6 * width), f32),
        pltpu.VMEM((1, extra * columns), f32),
    )[0]


def deal_again(pieces, count):
    steps = len(pieces)
    columns = pieces[0].shape[1]
    extra = pieces[0].shape[0] - GROUP

    def kernel(*refs):
        sums = refs[0][GROUP:, :]
        for m in range(1, steps):
            sums = sums + refs[m][GROUP:, :]
        refs[-1][...] = sums
        for d in range(GROUP):
            out = refs[steps + d]
            for m in range(steps):
                out[m : m + 1, :] = refs[m][d : d + 1, :]
            out[steps:, :] = sums[:count, :]

    outs = call(
        kernel,
        [((steps + count, columns), f32)] * GROUP + [((extra, columns), f32)],
        pieces,
    )
    return outs[:GROUP], outs[GROUP]


def split_four(value, place):
    rows = value.shape[0] // GROUP
    chunks = value.reshape(GROUP, rows, value.shape[1])

    def kernel(at, *refs):
        for d in range(GROUP):
            refs[1 + d][...] = refs[0][at[0] ^ d]

    return place_call(kernel, [((rows, value.shape[1]), bf16)] * GROUP, [chunks], place)


def row_sum(value):
    return jnp.sum(value, axis=0, keepdims=True)


def first_branch(parts, bias, inputs, gate, scale, shift):
    shape = inputs.shape

    def kernel(a, b, c, d, bi, x, g, sc, sh, branch_out, hidden_out, normed_out):
        branch = total_of((a, b, c, d)) + bi[...]
        hidden = x[...].astype(f32) + g[0:1, :] * branch
        branch_out[...] = branch
        hidden_out[...] = hidden
        normed_out[...] = (norm(hidden)[0] * (1.0 + sc[0:1, :]) + sh[0:1, :]).astype(bf16)

    return call(
        kernel,
        [(shape, f32), (shape, f32), (shape, bf16)],
        (*parts, bias, inputs, gate, scale, shift),
    )


def second_backward(parts, hidden, branch, cot, scale, gate):
    shape = hidden.shape

    def kernel(a, b, c, d, h, br, g, sc, gt, hidden_out, branch_out, sums):
        grad = total_of((a, b, c, d))
        normed, inverse = norm(h[...])
        grad_hidden = g[...].astype(f32) + norm_back(grad, normed, inverse, sc[0:1, :])
        hidden_out[...] = grad_hidden
        branch_out[...] = (gt[0:1, :] * grad_hidden).astype(bf16)
        sums[0:1, :] = row_sum(grad_hidden * br[...])
        sums[1:2, :] = row_sum(grad)
        sums[2:3, :] = row_sum(grad * normed)

    return call(
        kernel,
        [(shape, f32), (shape, bf16), ((3, shape[1]), f32)],
        (*parts, hidden, branch, cot, scale, gate),
    )


def second_branch(parts, bias, hidden, gate, cot):
    shape = hidden.shape

    def kernel(a, b, c, d, bi, h, gt, g, out, gate_sum):
        branch = total_of((a, b, c, d)) + bi[...]
        out[...] = (h[...] + gt[0:1, :] * branch).astype(bf16)
        gate_sum[...] = row_sum(g[...].astype(f32) * branch)

    return call(
        kernel, [(shape, bf16), ((1, shape[1]), f32)], (*parts, bias, hidden, gate, cot)
    )


def first_backward(parts, inputs, grad_hidden, scale, sums, gate_sum):
    shape = inputs.shape

    def kernel(a, b, c, d, x, gh, sc, s, gs, out, mod):
        grad = total_of((a, b, c, d))
        normed, inverse = norm(x[...].astype(f32))
        out[...] = (gh[...] + norm_back(grad, normed, inverse, sc[0:1, :])).astype(bf16)
        mod[0:1, :] = row_sum(grad)
        mod[1:2, :] = row_sum(grad * normed)
        mod[2:5, :] = s[...]
        mod[5:6, :] = gs[...]

    return call(
        kernel,
        [(shape, bf16), ((6, shape[1]), f32)],
        (*parts, inputs, grad_hidden, scale, sums, gate_sum),
    )


def head_masks(feats):
    lane = lax.broadcasted_iota(jnp.int32, (1, feats), 1)
    return [(lane >= h * HEAD) & (lane < (h + 1) * HEAD) for h in range(feats // HEAD)]


def only(mask, value):
    return jnp.where(mask, value, jnp.zeros_like(value))


def split_store(keep_ref, send_ref, value):
    half = value.shape[0] // 2
    keep_ref[...] = value[:half]
    send_ref[...] = value[half:].astype(bf16)


def attention_forward(near, far, shift, scale, weights, biases):
    total, width = 2 * near.shape[0], near.shape[1]
    feats = biases.shape[1]
    seq = total // GROUP
    factor = HEAD ** (-0.5)

    def kernel(t_near, t_far, sh, sc, w, b, normed, q_out, k_out, v_out, att, keep, send):
        for i in range(GROUP):
            rows = slice(i * seq, (i + 1) * seq)
            tok = t_near if i < GROUP // 2 else t_far
            value = norm(tok[i % 2 * seq : (i % 2 + 1) * seq, :].astype(f32))[0]
            normed[rows, :] = (value * (1.0 + sc[i : i + 1, :]) + sh[i : i + 1, :]).astype(bf16)
        projected = dot(normed[...], w[:, : 3 * feats])
        q_out[...] = (projected[:, :feats] + b[0:1, :]).astype(bf16)
        k_out[...] = projected[:, feats : 2 * feats].astype(bf16)
        v_out[...] = (projected[:, 2 * feats :] + b[1:2, :]).astype(bf16)
        masks = head_masks(feats)
        for i in range(GROUP):
            rows = slice(i * seq, (i + 1) * seq)
            q, k, v = q_out[rows, :], k_out[rows, :], v_out[rows, :]
            result = jnp.zeros((seq, feats), f32)
            for mask in masks:
                probs = softmax(dot_rows(only(mask, q), k) * factor)
                result += dot(probs.astype(bf16), only(mask, v))
            att[rows, :] = result.astype(bf16)
        split_store(keep, send, dot_rows(att[...], w[:, 3 * feats :]))

    return call(
        kernel,
        [
            ((total, width), bf16),
            ((total, feats), bf16),
            ((total, feats), bf16),
            ((total, feats), bf16),
            ((total, feats), bf16),
            ((total // 2, width), f32),
            ((total // 2, width), bf16),
        ],
        (near, far, shift, scale, weights, biases),
    )


def softmax(scores):
    exponent = jnp.exp(scores - jnp.max(scores, axis=-1, keepdims=True))
    return exponent / jnp.sum(exponent, axis=-1, keepdims=True)


def symmetric_sum(parts):
    pairs = [parts[2 * i] + parts[2 * i + 1] for i in range(GROUP)]
    return (pairs[0] + pairs[1]) + (pairs[2] + pairs[3])


def attention_backward(near, far, q_all, k_all, v_all, weights):
    total = q_all.shape[0]
    width, feats = weights.shape[0], q_all.shape[1]
    seq = total // GROUP
    factor = HEAD ** (-0.5)

    def kernel(g_near, g_far, q_in, k_in, v_in, w, grad_in, keep, send, bias, g, proj_bias):
        masks = head_masks(feats)
        g[: total // 2, :] = g_near[...]
        g[total // 2 :, :] = g_far[...]
        half = seq // 2
        proj_bias[...] = symmetric_sum(
            [row_sum(g[i * half : (i + 1) * half, :].astype(f32)) for i in range(2 * GROUP)]
        )
        grad_att = dot(g[...], w[:, 3 * feats :]).astype(bf16)
        q_sum = jnp.zeros((1, feats), f32)
        v_sum = jnp.zeros((1, feats), f32)
        for i in range(GROUP):
            rows = slice(i * seq, (i + 1) * seq)
            q, k, v = q_in[rows, :], k_in[rows, :], v_in[rows, :]
            ga = grad_att[rows, :]
            gq = jnp.zeros((seq, feats), f32)
            gk = jnp.zeros((seq, feats), f32)
            gv = jnp.zeros((seq, feats), f32)
            for mask in masks:
                probs = softmax(dot_rows(only(mask, q), k) * factor)
                gv += only(mask, transposed_dot(probs.astype(bf16), ga))
                gp = dot_rows(only(mask, ga), v)
                gs = probs * (gp - jnp.sum(probs * gp, axis=-1, keepdims=True))
                gs = gs.astype(bf16)
                gq += only(mask, dot(gs, k))
                gk += only(mask, transposed_dot(gs, q))
            gq, gk = gq * factor, gk * factor
            q_sum += jnp.sum(gq, axis=0, keepdims=True)
            v_sum += jnp.sum(gv, axis=0, keepdims=True)
            grad_in[rows, :] = jnp.concatenate([gq, gk, gv], axis=1).astype(bf16)
        bias[0:1, :] = q_sum
        bias[1:2, :] = v_sum
        split_store(keep, send, dot_rows(grad_in[...], w[:, : 3 * feats]))

    return call(
        kernel,
        [
            ((total, 3 * feats), bf16),
            ((total // 2, width), f32),
            ((total // 2, width), bf16),
            ((2, feats), f32),
            ((total, width), bf16),
            ((1, width), f32),
        ],
        (near, far, q_all, k_all, v_all, weights),
    )


def attention_weights(grad_in, normed, grad_branch, att):
    width, feats = normed.shape[1], att.shape[1]

    def kernel(gi, n, g, a, grads):
        grads[:, : 3 * feats] = transposed_dot(n[...], gi[...]).astype(bf16)
        grads[:, 3 * feats :] = transposed_dot(g[...], a[...]).astype(bf16)

    return call(kernel, [((width, 4 * feats), bf16)], (grad_in, normed, grad_branch, att))[0]


def feed_forward(near, far, weights, bias, cot_near, cot_far, gate):
    total, width = 2 * near.shape[0], near.shape[1]
    units = weights.shape[1] // 2
    seq = total // GROUP

    def kernel(
        n_near, n_far, w, b, c_near, c_far, gt, grads, pre_out, act_out, bias_out, fc2_out, grad_out, n
    ):
        n[: total // 2, :] = n_near[...]
        n[total // 2 :, :] = n_far[...]
        sums = []
        half = seq // 2
        for i in range(2 * GROUP):
            c = c_near if i < GROUP else c_far
            value = c[i % GROUP * half : (i % GROUP + 1) * half, :].astype(f32)
            value = value * gt[i // 2 : i // 2 + 1, :]
            sums.append(row_sum(value))
            grad_out[i * half : (i + 1) * half, :] = value.astype(bf16)
        fc2_out[...] = symmetric_sum(sums)
        pre = dot(n[...], w[:, :units]) + b[...]
        inner = ROOT * (pre + 0.044715 * (pre * pre * pre))
        tanh = jnp.tanh(inner)
        act = (0.5 * pre * (1.0 + tanh)).astype(bf16)
        slope = 0.5 * (1.0 + tanh) + 0.5 * pre * (1.0 - tanh * tanh) * (
            ROOT * (1.0 + 3 * 0.044715 * (pre * pre))
        )
        grad_pre = dot(grad_out[...], w[:, units:]) * slope
        bias_out[...] = jnp.sum(grad_pre, axis=0, keepdims=True)
        grad_pre = grad_pre.astype(bf16)
        grads[:, units:] = transposed_dot(grad_out[...], act).astype(bf16)
        grads[:, :units] = transposed_dot(n[...], grad_pre).astype(bf16)
        pre_out[...] = grad_pre
        act_out[...] = act

    return call(
        kernel,
        [
            ((width, 2 * units), bf16),
            ((total, units), bf16),
            ((total, units), bf16),
            ((1, units), f32),
            ((1, width), f32),
        ],
        (near, far, weights, bias, cot_near, cot_far, gate),
        pltpu.VMEM((total, width), bf16),
        pltpu.VMEM((total, width), bf16),
    )


def feed_forward_rows(value, weights, start):
    total, units = value.shape
    width = weights.shape[0]

    def kernel(a, w, keep, send):
        split_store(keep, send, dot_rows(a[...], w[:, start : start + units]))

    return call(
        kernel,
        [((total // 2, width), f32), ((total // 2, width), bf16)],
        (value, weights),
    )


def local(
    tokens,
    conditions,
    mod_weight,
    mod_bias,
    qkv_weight,
    qv_bias,
    proj_weight,
    proj_bias,
    fc1_weight,
    fc1_bias,
    fc2_weight,
    fc2_bias,
    cotangent,
):
    seq, width = tokens.shape
    rows = seq // 2
    d_rows = qkv_weight.shape[0]
    t_width = qkv_weight.shape[2]
    hidden = fc1_weight.shape[1]
    feats = t_width // GROUP
    units = hidden // GROUP
    n_dp = width // d_rows
    t = lax.axis_index("tensor")
    place = lax.axis_index("xx") * 2 + lax.axis_index("core")
    dp = lax.axis_index("zz") * GROUP + place

    attn_arrays = [qkv_weight.transpose(1, 0, 2), proj_weight.T]
    attn_part = join(send_four(pack(attn_arrays, place)), place)
    attn_full = lax.all_gather(attn_part, "zz", axis=0, tiled=True)

    cond_values = conditions.astype(f32)
    silu_conds = jax.nn.silu(cond_values).astype(bf16)
    small = jnp.concatenate(
        [silu_conds, qv_bias, proj_bias[None], fc1_bias, fc2_bias[None]], axis=1
    )
    small = gather_dp(after(small, attn_part))
    all_silu = small[:, :width]
    spots = jnp.arange(n_dp)
    order = ((spots[:, None] ^ dp) == spots[None]).astype(bf16)
    biases = product(order, small[:, width:], "ij,jc->ic")
    n_qv, n_b, n_f = qv_bias.shape[1], proj_bias.shape[0], fc1_bias.shape[1]
    cuts = [n_qv, n_qv + n_b, n_qv + n_b + n_f]
    qv_full = biases[:, : cuts[0]].reshape(2, GROUP, feats)
    proj_bias_full = biases[:, cuts[0] : cuts[1]].reshape(width)
    fc1_bias_full = biases[:, cuts[1] : cuts[2]].reshape(GROUP, units)
    fc2_bias_full = biases[:, cuts[2] :].reshape(width)
    qv_here = lax.dynamic_index_in_dim(qv_full, place, 1, keepdims=False)
    fc1_bias_here = lax.dynamic_index_in_dim(fc1_bias_full, place, 0, keepdims=False)
    mod_columns = product(all_silu, mod_weight, "ld,dc->lc") + mod_bias.astype(f32)
    n_zz = n_dp // GROUP
    mod_parts = send_zz([mod_columns[m * GROUP : (m + 1) * GROUP] for m in range(n_zz)])
    mod_parts = after(jnp.stack(mod_parts), attn_full)
    mod_parts = send_four([mod_parts] * GROUP)
    modulation = collect_rows(mod_parts, dp, width)
    shift_attn, scale_attn, gate_attn, shift_mlp, scale_mlp, gate_mlp = modulation
    mlp_arrays = [fc1_weight, fc2_weight.T]
    mlp_part = join(send_four(pack(mlp_arrays, place)), place)
    mlp_full = lax.all_gather(mlp_part, "zz", axis=0, tiled=True)
    def own_order(value):
        first = lax.dynamic_slice_in_dim(value, t * rows, rows, 0)
        second = lax.dynamic_slice_in_dim(value, (1 - t) * rows, rows, 0)
        return jnp.concatenate([first, second], axis=0)

    def true_order(own, other):
        return jnp.where(
            t == 0,
            jnp.concatenate([own, other], axis=0),
            jnp.concatenate([other, own], axis=0),
        )

    tokens_own = own_order(tokens)
    cot_own = after(own_order(cotangent), mod_columns)
    tokens_near, tokens_far = gather_four(tokens_own)
    cot_near, cot_far = gather_four(cot_own)
    inputs_half = tokens_own[:rows]
    grad_out_half = cot_own[:rows]

    normed_one, queries, keys, values, attended, keep, send = attention_forward(
        tokens_near, tokens_far, shift_attn, scale_attn, attn_full, qv_here
    )
    branch_half, hidden_half, normed_two_half = first_branch(
        scatter_eight(keep, send),
        proj_bias_full[None],
        inputs_half,
        gate_attn,
        scale_mlp,
        shift_mlp,
    )

    normed_two_half = after(normed_two_half, cot_far)
    near, far = gather_eight(normed_two_half)
    mlp_grad, grad_pre, activated, fc1_bias_part, fc2_bias_part = feed_forward(
        near, far, mlp_full, fc1_bias_here[None], cot_near, cot_far, gate_mlp
    )
    mlp_grad = lax.psum_scatter(mlp_grad, "zz", scatter_dimension=0, tiled=True)
    keep, send = feed_forward_rows(grad_pre, mlp_full, 0)
    grad_hidden_half, grad_branch_half, mod_sums = second_backward(
        scatter_eight(keep, send), hidden_half, branch_half, grad_out_half, scale_mlp, gate_attn
    )
    near, far = gather_eight(grad_branch_half)

    grad_in, keep, send, qv_bias_part, grad_branch_all, proj_bias_part = attention_backward(
        near, far, queries, keys, values, attn_full
    )

    out_keep, out_send = feed_forward_rows(
        after(activated, grad_branch_half), mlp_full, units
    )
    block_half, gate_sum = second_branch(
        scatter_eight(out_keep, out_send),
        fc2_bias_full[None],
        hidden_half,
        gate_mlp,
        grad_out_half,
    )

    attn_grads = attention_weights(
        after(grad_in, gate_sum), normed_one, grad_branch_all, attended
    )
    attn_grads = after(attn_grads, mlp_grad)
    attn_grad = lax.psum_scatter(attn_grads, "zz", scatter_dimension=0, tiled=True)
    tokens_grad_half, grad_mod = first_backward(
        scatter_eight(keep, after(send, attn_grads)),
        inputs_half,
        grad_hidden_half,
        scale_attn,
        mod_sums,
        gate_sum,
    )

    block_out = true_order(block_half, exchange(block_half, "tensor"))
    tokens_grad = true_order(tokens_grad_half, exchange(tokens_grad_half, "tensor")).astype(f32)
    mlp_parts = send_four(split_four(mlp_grad, place))
    fc1_weight_grad, fc2_weight_grad = unpack(mlp_parts, (1, 1), place)
    grad_mod_other = exchange(after(grad_mod, fc1_weight_grad), "tensor")
    own = 2 * feats + units
    bias_parts = (qv_bias_part, fc1_bias_part, proj_bias_part, fc2_bias_part)
    dealt = deal_columns(grad_mod, grad_mod_other, bias_parts, dp, n_zz)
    own_rows = -(-own // dealt.shape[2])
    dealt = send_zz([dealt[m] for m in range(n_zz)])
    attn_parts = split_four(after(attn_grad, fc1_weight_grad), place)
    dealt, biases = deal_again(dealt, own_rows)
    dealt = send_four(dealt)
    dealt = jnp.stack([after(dealt[0], attn_parts[0])] + dealt[1:], axis=1)
    grad_mod_columns = dealt[:n_zz].reshape(n_dp, dealt.shape[2]).astype(bf16)
    mod_bias_grad = jnp.sum(grad_mod_columns.astype(f32), axis=0)
    grad_silu = product(grad_mod_columns, mod_weight, "lc,dc->ld")
    attn_parts = send_four(attn_parts)
    qkv_weight_grad, proj_weight_grad = unpack(attn_parts, (3, 1), place)
    grad_silu, near_sum = scatter_dp(grad_silu, proj_weight_grad)
    mod_weight_grad = product(all_silu, after(grad_mod_columns, near_sum), "ld,lc->dc")
    conditions_grad = jax.vjp(jax.nn.silu, cond_values)[1](grad_silu)[0]

    biases = biases.reshape(-1)
    group_biases = dealt[n_zz:].transpose(1, 0, 2).reshape(GROUP, -1)[:, :own]
    group_biases = reorder(group_biases, place)
    qv_all = jnp.concatenate(
        [group_biases[:, :feats].reshape(-1), group_biases[:, feats : 2 * feats].reshape(-1)]
    )
    fc1_all = group_biases[:, 2 * feats :].reshape(-1)
    proj_all = biases[own : own + width]
    fc2_all = biases[own + width : own + 2 * width]

    def piece(vector):
        size = vector.shape[0] // n_dp
        return lax.dynamic_slice_in_dim(vector, dp * size, size, 0)

    qkv_weight_grad = qkv_weight_grad.transpose(1, 0, 2)
    fc1_weight_grad = fc1_weight_grad[0]
    fc2_weight_grad = fc2_weight_grad[0].T
    proj_weight_grad = proj_weight_grad[0].T
    return (
        block_out,
        tokens_grad,
        conditions_grad,
        mod_weight_grad,
        mod_bias_grad,
        qkv_weight_grad,
        piece(qv_all)[None],
        proj_weight_grad,
        piece(proj_all),
        fc1_weight_grad,
        piece(fc1_all)[None],
        fc2_weight_grad,
        piece(fc2_all),
    )


def solution(mesh):
    n_dp, n_tensor = mesh.shape["dp"], mesh.shape["tensor"]
    cut = Mesh(
        mesh.devices.reshape(n_dp // GROUP, 2, 2, n_tensor), ("zz", "xx", "core", "tensor")
    )
    dp = ("zz", "xx", "core")
    return jax.shard_map(
        local,
        mesh=cut,
        in_specs=(
            P(dp, None),
            P(dp, None),
            P(None, dp),
            P(dp),
            P(dp, None, "tensor"),
            P("tensor", dp),
            P("tensor", dp),
            P(dp),
            P(dp, "tensor"),
            P("tensor", dp),
            P("tensor", dp),
            P(dp),
            P(dp, None),
        ),
        out_specs=(
            P(dp, None),
            P(dp, None),
            P(dp, None),
            P(None, dp),
            P(dp),
            P(dp, None, "tensor"),
            P("tensor", dp),
            P("tensor", dp),
            P(dp),
            P(dp, "tensor"),
            P("tensor", dp),
            P("tensor", dp),
            P(dp),
        ),
        check_vma=False,
    )
```
